32 devices in a mesh: dp: 2 (over core), lat: 4 (over z), lon: 4 (over y, x).
Axes of the slice: x: 2, y: 2, z: 4, core: 2. Of those that a mesh axis runs over, the one named last changes fastest.
Arguments:
- fields: bfloat16 [2, 320, 512, 128], P('dp', 'lat', 'lon'), may hold values from -6 to 6
- down_weight: bfloat16 [3, 3, 128, 128], P(None, None, 'dp'), may hold values from -0.1875 to 0.1875
- mid_weight: bfloat16 [3, 3, 128, 128], P(None, None, 'dp'), may hold values from -0.1875 to 0.1875
- up_weight: bfloat16 [3, 3, 128, 128], P(None, None, 'dp'), may hold values from -0.1875 to 0.1875
- cotangent: bfloat16 [2, 320, 512, 128], P('dp', 'lat', 'lon'), may hold values from -6 to 6
Outputs:
- level_out: bfloat16 [2, 320, 512, 128], P('dp', 'lat', 'lon')
- grad_fields: bfloat16 [2, 320, 512, 128], P('dp', 'lat', 'lon')
- grad_down: float32 [3, 3, 128, 128], P(None, None, 'dp')
- grad_mid: float32 [3, 3, 128, 128], P(None, None, 'dp')
- grad_up: float32 [3, 3, 128, 128], P(None, None, 'dp')
The draws below stay inside these ranges and needn't reach their ends.
All inputs are finite; a program needn't handle non-finite values.
Results may differ from the reference program's by a relative error of at most 0.012.
Values may be sent and summed in bfloat16 or wider, within the bound.
A program may use at most 128 MiB of HBM per device.

```python
import math
import jax
import jax.numpy as jnp
from jax import lax

CHANNELS = 128
MEMBERS = 2
GRID_LAT = 320
GRID_LON = 512


def level_of(own_key, extent, split, least, largest):
    loudness = 1.0
    for axis_at, blocks in split:
        heights = jax.random.uniform(jax.random.fold_in(jax.random.fold_in(own_key, 6), axis_at), (blocks,), jnp.float32, least / len(split), largest / len(split))
        loudness = loudness * jnp.repeat(jnp.exp(heights), extent[axis_at] // blocks).reshape((-1,) + (1,) * (len(extent) - 1 - axis_at))
    return loudness


def bell_draw(stream_key, shape, spread, most, cuts=(), held_as=jnp.bfloat16):
    values = jax.random.normal(stream_key, shape, jnp.float32) * spread
    if len(cuts) > 0:
        values = level_of(stream_key, shape, cuts, -0.22, 0.18) * values
    return jnp.clip(values, min=-most, max=most).astype(held_as)


def setup_inputs(seed: int = 0) -> dict:
    keys = jax.random.split(jax.random.key(seed), 6)
    fields = bell_draw(keys[0], (MEMBERS, GRID_LAT, GRID_LON, CHANNELS), 1.0, 6.0, ((0, 2), (1, 4), (2, 4)))
    down_weight = bell_draw(keys[1], (3, 3, CHANNELS, CHANNELS), (9 * CHANNELS) ** -0.5, 0.1875, ((2, 2),))
    mid_weight = bell_draw(keys[2], (3, 3, CHANNELS, CHANNELS), (9 * CHANNELS) ** -0.5, 0.1875, ((2, 2),))
    up_weight = bell_draw(keys[3], (3, 3, CHANNELS, CHANNELS), (9 * CHANNELS) ** -0.5, 0.1875, ((2, 2),))
    cotangent = bell_draw(keys[4], (MEMBERS, GRID_LAT, GRID_LON, CHANNELS), 1.0, 6.0, ((0, 2), (1, 4), (2, 4)))
    return dict(fields=fields, down_weight=down_weight, mid_weight=mid_weight, up_weight=up_weight, cotangent=cotangent)


RULE = (((1, 0),), ((0, 1), (2, 0)))

def frame(field):
    tall = jnp.pad(field, ((0, 0), (1, 1), (0, 0), (0, 0)))
    return jnp.concatenate([tall[:, :, -1:], tall, tall[:, :, :1]], axis=2)

def apply_tap(piece, kernel):
    flat = piece.reshape(-1, piece.shape[-1]).astype(jnp.float32)
    result = jnp.dot(flat, kernel.astype(jnp.float32), preferred_element_type=jnp.float32)
    return result.reshape(piece.shape[:-1] + (kernel.shape[1],))

def outer_sum(left, right):
    flat_left = left.reshape(-1, left.shape[-1]).astype(jnp.float32)
    flat_right = right.reshape(-1, right.shape[-1]).astype(jnp.float32)
    return jnp.dot(flat_left.T, flat_right, preferred_element_type=jnp.float32)

def taps_down(padded, kernel):
    half_rows = (padded.shape[1] - 2) // 2
    half_cols = (padded.shape[2] - 2) // 2
    total = 0.0
    for row in range(3):
        for col in range(3):
            piece = padded[:, row:row + 2 * half_rows:2, col:col + 2 * half_cols:2]
            total = total + apply_tap(piece, kernel[row, col])
    return total

def taps_same(padded, kernel):
    rows = padded.shape[1] - 2
    cols = padded.shape[2] - 2
    total = 0.0
    for row in range(3):
        for col in range(3):
            total = total + apply_tap(padded[:, row:row + rows, col:col + cols], kernel[row, col])
    return total

def taps_up(padded, kernel):
    rows = padded.shape[1] - 2
    cols = padded.shape[2] - 2
    phase_rows = []
    for alpha in range(2):
        phase_cols = []
        for beta in range(2):
            total = 0.0
            for row, row_off in RULE[alpha]:
                for col, col_off in RULE[beta]:
                    piece = padded[:, 1 + row_off:1 + row_off + rows, 1 + col_off:1 + col_off + cols]
                    total = total + apply_tap(piece, kernel[row, col])
            phase_cols.append(total)
        phase_rows.append(jnp.stack(phase_cols, axis=3))
    whole = jnp.stack(phase_rows, axis=2)
    return whole.reshape(whole.shape[0], 2 * rows, 2 * cols, whole.shape[-1])

def grad_down_taps(padded, grad):
    half_rows = grad.shape[1]
    half_cols = grad.shape[2]
    table = []
    for row in range(3):
        line = []
        for col in range(3):
            piece = padded[:, row:row + 2 * half_rows:2, col:col + 2 * half_cols:2]
            line.append(outer_sum(piece, grad))
        table.append(jnp.stack(line))
    return jnp.stack(table)

def grad_same_taps(padded, grad):
    rows = grad.shape[1]
    cols = grad.shape[2]
    table = []
    for row in range(3):
        line = []
        for col in range(3):
            line.append(outer_sum(padded[:, row:row + rows, col:col + cols], grad))
        table.append(jnp.stack(line))
    return jnp.stack(table)

def grad_up_taps(padded, grad):
    rows = padded.shape[1] - 2
    cols = padded.shape[2] - 2
    entries = {}
    for alpha in range(2):
        for beta in range(2):
            phase = grad[:, alpha::2, beta::2]
            for row, row_off in RULE[alpha]:
                for col, col_off in RULE[beta]:
                    piece = padded[:, 1 + row_off:1 + row_off + rows, 1 + col_off:1 + col_off + cols]
                    entries[row, col] = outer_sum(piece, phase)
    return jnp.stack([jnp.stack([entries[row, col] for col in range(3)]) for row in range(3)])

def swap_io(kernel):
    return jnp.transpose(kernel, (0, 1, 3, 2))

def one_member(pair):
    fields, cotangent, down_weight, mid_weight, up_weight = pair
    fields = fields[None]
    cotangent = cotangent[None]
    framed_in = frame(fields)
    down = taps_down(framed_in, down_weight).astype(jnp.bfloat16)
    framed_down = frame(down)
    pre = taps_same(framed_down, mid_weight)
    mid = jax.nn.silu(pre).astype(jnp.bfloat16)
    framed_mid = frame(mid)
    level_out = (fields.astype(jnp.float32) + taps_up(framed_mid, up_weight)).astype(jnp.bfloat16)
    framed_cot = frame(cotangent)
    grad_mid_map = taps_down(framed_cot, swap_io(up_weight))
    sig = jax.nn.sigmoid(pre)
    grad_pre = (grad_mid_map * sig * (1.0 + pre * (1.0 - sig))).astype(jnp.bfloat16)
    grad_down_map = taps_same(frame(grad_pre), swap_io(mid_weight)[::-1, ::-1]).astype(jnp.bfloat16)
    grad_fields = (cotangent.astype(jnp.float32) + taps_up(frame(grad_down_map), swap_io(down_weight))).astype(jnp.bfloat16)
    up_term = grad_up_taps(framed_mid, cotangent)
    mid_term = grad_same_taps(framed_down, grad_pre)
    down_term = grad_down_taps(framed_in, grad_down_map)
    return (level_out[0], grad_fields[0], down_term, mid_term, up_term)

def reference(fields, down_weight, mid_weight, up_weight, cotangent):

    def member_step(pair):
        return one_member((pair[0], pair[1], down_weight, mid_weight, up_weight))
    level_out, grad_fields, down_terms, mid_terms, up_terms = lax.map(member_step, (fields, cotangent))
    scale = 1.0 / math.sqrt(MEMBERS * GRID_LAT * GRID_LON)
    grad_down = lax.optimization_barrier(jnp.sum(down_terms, axis=0)) * scale
    grad_mid = lax.optimization_barrier(jnp.sum(mid_terms, axis=0)) * scale
    grad_up = lax.optimization_barrier(jnp.sum(up_terms, axis=0)) * scale
    return (level_out, grad_fields, grad_down, grad_mid, grad_up)
```

```python
import functools
import math

import jax
import jax.numpy as jnp
from jax import lax
from jax.experimental import pallas as pl
from jax.experimental.pallas import tpu as pltpu
from jax.sharding import PartitionSpec as P

EDGE = 8
BF = jnp.bfloat16
F32 = jnp.float32


def dot(a, b):
    return lax.dot_general(a, b, (((1,), (0,)), ((), ())), preferred_element_type=F32)


def dot_t(a, b):
    return lax.dot_general(a, b, (((0,), (0,)), ((), ())), preferred_element_type=F32)


def rolled(x, by):
    return pltpu.roll(x, by % x.shape[0], 0)


def lanes(*parts):
    return jnp.concatenate(parts, axis=-1)


def blocks(rows):
    return jnp.concatenate([lanes(*row) for row in rows], axis=0)


def strided_block(w, r, z):
    return blocks([[w(r, 1), z], [w(r, 2), w(r, 0)]])


def spread_block(w, r, z):
    return blocks([[w(r, 1), w(r, 2)], [z, w(r, 0)]])


def paired_block(w, c, z):
    return blocks([[w(0, c), z], [w(1, c), w(0, c)], [w(2, c), w(1, c)], [z, w(2, c)]])


def flat(x):
    return x.reshape(x.shape[0] * x.shape[1], x.shape[2])


def compute(half, scale, f, c, wd, wm, wu, out, gout, grads,
            bd, bg, bm, bn, bu, bf, dp, gps, gpp, s1, s2, acc_u, acc_m, acc_d):
    wide = f.shape[2]
    ch = f.shape[3] // 2
    cols = wide - 2 * EDGE
    z = jnp.zeros((ch, ch), BF)
    lat = lax.axis_index("lat")
    first = lat == 0
    last = lat == lax.axis_size("lat") - 1
    low = jnp.where(first, 0, -(1 << 20))
    high = jnp.where(last, half, 1 << 20)

    def plain(ref):
        return lambda r, k: ref[r, k]

    def turned(ref):
        return lambda r, k: ref[r, k].T

    def flipped(ref):
        return lambda r, k: ref[2 - r, 2 - k].T

    for r in range(3):
        at = pl.ds(2 * ch * r, 2 * ch)
        bd[at, :] = strided_block(plain(wd), r, z)
        bg[at, :] = strided_block(turned(wu), r, z)
        bu[at, :] = spread_block(plain(wu), r, z)
        bf[at, :] = spread_block(turned(wd), r, z)
        bm[:, at] = paired_block(plain(wm), r, z)
        bn[:, at] = paired_block(flipped(wm), r, z)

    def inside(rows):
        return jnp.logical_and(rows >= low, rows < high)

    def row_mask(n, base, shape_cols):
        rows = base + lax.broadcasted_iota(jnp.int32, (n, wide, shape_cols), 0)
        return inside(rows)

    def pair_mask(n, base):
        shape = (n, wide, 2 * ch)
        rows = (base + 2 * lax.broadcasted_iota(jnp.int32, shape, 0)
                + (lax.broadcasted_iota(jnp.int32, shape, 2) >= ch).astype(jnp.int32))
        return inside(rows)

    def strided(src, start, n, weight):
        x0 = src[pl.ds(start, n), 1]
        x1 = src[pl.ds(start + 1, n), 0]
        x2 = src[pl.ds(start + 1, n), 1]
        acc = dot(flat(lanes(x0, x1, x2)), weight[...])
        return acc[:, :ch] + rolled(acc[:, ch:], 1)

    def to_pairs(x, n):
        x = x.reshape(n, 2, wide, ch)
        return lanes(x[:, 0], x[:, 1])

    def same(src, start, n, weight):
        acc = dot(flat(lanes(src[pl.ds(start, n)], src[pl.ds(start + 1, n)])), weight[...])
        k = 2 * ch
        total = rolled(acc[:, :k], 1) + acc[:, k:2 * k] + rolled(acc[:, 2 * k:], -1)
        return total

    pairs = (half + 8) // 2
    nd = 6 if pairs % 6 == 0 else 1

    def down_step(t, _):
        q = t * nd
        v = strided(f, 2 * q, 2 * nd, bd)
        v = to_pairs(v, nd)
        dp[pl.ds(q, nd)] = jnp.where(pair_mask(nd, 2 * q - 3), v, 0.0).astype(BF)
        return 0

    lax.fori_loop(0, pairs // nd, down_step, 0)

    def shifted_rows(dst, start, n, v):
        nxt = rolled(v, -1)
        for a in range(2):
            half_lanes = slice(a * ch, (a + 1) * ch)
            piece = lanes(v[:, half_lanes], nxt[:, half_lanes]).astype(BF)
            dst[pl.ds(start, n), a] = piece.reshape(n, wide, 2 * ch)

    pairs_mid = (half + 4) // 2
    nm = 11 if pairs_mid % 11 == 0 else 1

    def mid_step(t, _):
        p = t * nm
        pre = same(dp, p, nm, bm)
        g = strided(c, 2 * p + 1, 2 * nm, bg)
        g = flat(to_pairs(g, nm))
        sig = jax.nn.sigmoid(pre)
        ok = flat(pair_mask(nm, 2 * p - 2))
        mid = jnp.where(ok, pre * sig, 0.0)
        gp = jnp.where(ok, g * sig * (1.0 + pre * (1.0 - sig)), 0.0)
        shifted_rows(s1, p, nm, mid)
        gpp[pl.ds(p, nm)] = gp.astype(BF).reshape(nm, wide, 2 * ch)
        place = lax.broadcasted_iota(jnp.int32, (nm, wide, 2 * ch), 1)
        own = flat(jnp.logical_and(place >= EDGE, place < EDGE + cols))
        gm = jnp.where(own, gp, 0.0)
        after, before = rolled(gm, -1), rolled(gm, 1)
        for a in range(2):
            k = slice(a * ch, (a + 1) * ch)
            piece = lanes(after[:, k], gm[:, k], before[:, k]).astype(BF)
            gps[pl.ds(p, nm), a] = piece.reshape(nm, wide, 3 * ch)
        return 0

    lax.fori_loop(0, pairs_mid // nm, mid_step, 0)

    pairs_gd = (half + 2) // 2
    ng = 7 if pairs_gd % 7 == 0 else 1

    def gd_step(t, _):
        q = t * ng
        v = same(gpp, q, ng, bn)
        v = jnp.where(flat(pair_mask(ng, 2 * q - 1)), v, 0.0)
        shifted_rows(s2, q, ng, v)
        return 0

    lax.fori_loop(0, pairs_gd // ng, gd_step, 0)

    acc_u[...] = jnp.zeros_like(acc_u)
    acc_m[...] = jnp.zeros_like(acc_m)
    acc_d[...] = jnp.zeros_like(acc_d)
    place = lax.broadcasted_iota(jnp.int32, (wide, 2 * ch), 0)
    place = place + (lax.broadcasted_iota(jnp.int32, (wide, 2 * ch), 1) >= ch).astype(jnp.int32)
    own = jnp.logical_and(place >= EDGE, place < EDGE + cols).astype(F32).astype(BF)[None]
    step = 4

    def taps(src, i, n):
        return flat(lanes(src[pl.ds(i + 3, n), 1], src[pl.ds(i + 4, n), 0], src[pl.ds(i + 4, n), 1]))

    def grads_step(t, _):
        p = t * step
        n = 2 * step
        i = 2 * p
        m = s1[pl.ds(p + 1, step)].reshape(n, wide, 2 * ch) * own
        acc_u[...] += dot_t(flat(m), taps(c, i, n))
        ga = s2[pl.ds(p, step + 1)].reshape(2 * step + 2, wide, 2 * ch)[1:1 + n] * own
        acc_d[...] += dot_t(flat(ga), taps(f, i, n))
        d0, d1 = dp[pl.ds(p + 1, step)], dp[pl.ds(p + 2, step)]
        acc_m[...] += (
            dot_t(flat(gps[pl.ds(p + 1, step), 0]), flat(lanes(d0, d1[:, :, :ch])))
            + dot_t(flat(gps[pl.ds(p + 1, step), 1]), flat(lanes(d0[:, :, ch:], d1)))
        )
        return 0

    lax.fori_loop(0, half // (2 * step), grads_step, 0)

    for r in range(3):
        for k in range(3):
            top = ch if k == 0 else 0
            left = 2 * ch * r + (0 if k == 1 else ch)
            tap = 3 * r + k
            grads[tap] = (acc_d[top:top + ch, left:left + ch] * scale).T.astype(BF)
            grads[9 + tap] = (acc_m[k * ch:(k + 1) * ch, r * ch:(r + 1) * ch] * scale).T.astype(BF)
            grads[18 + tap] = (acc_u[top:top + ch, left:left + ch] * scale).astype(BF)

    def up_step(t, _):
        i = t * n_up
        def rows1(at, n):
            q = t * (n_up // 2) + 1
            return s1[pl.ds(q, n // 2 + 1)].reshape(n + 2, wide, 2 * ch)[at:at + n]
        def rows2(at, n):
            q = t * (n_up // 2)
            return s2[pl.ds(q, n // 2 + 1)].reshape(n + 2, wide, 2 * ch)[at + 1:at + 1 + n]
        for rows, base, dst, weight in ((rows1, f, out, bu), (rows2, c, gout, bf)):
            lo, hi = flat(rows(0, n_up)), flat(rows(1, n_up))
            k = 2 * ch
            even = dot(lo, weight[k:2 * k, :])
            odd = dot(lo, weight[2 * k:, :]) + dot(hi, weight[:k, :])
            for a, v in enumerate((even, odd)):
                v = v.reshape(n_up, wide, k) + base[pl.ds(i + 4, n_up), a].astype(F32)
                dst[pl.ds(i, n_up), a] = v[:, EDGE:EDGE + cols].astype(BF)
        return 0

    n_up = 8
    lax.fori_loop(0, half // n_up, up_step, 0)


def shifted(x, axis, width, dim, periodic):
    count = lax.axis_size(axis)
    forward = [(i, i + 1) for i in range(count - 1)]
    if periodic:
        forward.append((count - 1, 0))
    backward = [(b, a) for a, b in forward]
    low = lax.ppermute(lax.slice_in_dim(x, x.shape[dim] - width, None, axis=dim), axis, forward)
    high = lax.ppermute(lax.slice_in_dim(x, 0, width, axis=dim), axis, backward)
    return low, high


def body(fields, down_weight, mid_weight, up_weight, cotangent):
    _, rows, full, ch = fields.shape
    half, cols = rows // 2, full // 2
    wide = cols + 2 * EDGE
    weights = jnp.stack([down_weight, mid_weight, up_weight])
    weights = lax.all_gather(weights, "dp", axis=3, tiled=True)
    cells = (lax.axis_size("dp") * rows * lax.axis_size("lat") * full * lax.axis_size("lon"))
    scale = 1.0 / math.sqrt(cells)
    x = jnp.stack([fields[0], cotangent[0]]).reshape(2, rows, cols, 2 * ch)
    low, high = shifted(x, "lat", 8, 1, False)
    tall = jnp.concatenate([low, x, high, jnp.zeros((2, 2, cols, 2 * ch), BF)], axis=1)
    low, high = shifted(tall, "lon", 4, 2, True)
    gap = jnp.zeros((2, rows + 18, EDGE - 4, 2 * ch), BF)
    whole = jnp.concatenate([gap, low, tall, high, gap], axis=2)
    whole = whole.reshape(2, half + 9, 2, wide, 2 * ch)
    k = 2 * ch
    vm = pl.BlockSpec(memory_space=pltpu.VMEM)
    out, gout, grads = pl.pallas_call(
        functools.partial(compute, half, scale),
        out_shape=(
            jax.ShapeDtypeStruct((half, 2, cols, k), BF),
            jax.ShapeDtypeStruct((half, 2, cols, k), BF),
            jax.ShapeDtypeStruct((27, ch, ch), BF),
        ),
        in_specs=[vm] * 5,
        out_specs=(vm, vm, vm),
        scratch_shapes=[
            pltpu.VMEM((3 * k, k), BF),
            pltpu.VMEM((3 * k, k), BF),
            pltpu.VMEM((2 * k, 3 * k), BF),
            pltpu.VMEM((2 * k, 3 * k), BF),
            pltpu.VMEM((3 * k, k), BF),
            pltpu.VMEM((3 * k, k), BF),
            pltpu.VMEM(((half + 8) // 2, wide, k), BF),
            pltpu.VMEM(((half + 4) // 2, 2, wide, 3 * ch), BF),
            pltpu.VMEM(((half + 4) // 2, wide, k), BF),
            pltpu.VMEM(((half + 4) // 2, 2, wide, k), BF),
            pltpu.VMEM(((half + 2) // 2, 2, wide, k), BF),
            pltpu.VMEM((k, 3 * k), F32),
            pltpu.VMEM((3 * ch, 3 * ch), F32),
            pltpu.VMEM((k, 3 * k), F32),
        ],
        compiler_params=pltpu.CompilerParams(vmem_limit_bytes=50 << 20),
    )(whole[0], whole[1], weights[0], weights[1], weights[2])
    mine = lax.psum_scatter(grads, "dp", scatter_dimension=1, tiled=True)
    total = lax.psum(mine.astype(F32), ("lat", "lon"))
    total = total.reshape(3, 3, 3, ch // lax.axis_size("dp"), ch)
    return (
        out.reshape(1, rows, full, ch),
        gout.reshape(1, rows, full, ch),
        total[0],
        total[1],
        total[2],
    )


def solution(mesh):
    maps = P("dp", "lat", "lon", None)
    kernel = P(None, None, "dp", None)
    return jax.shard_map(
        body,
        mesh=mesh,
        in_specs=(maps, kernel, kernel, kernel, maps),
        out_specs=(maps, maps, kernel, kernel, kernel),
        check_vma=False,
    )
```

```python
import functools
import math

import jax
import jax.numpy as jnp
from jax import lax
from jax.experimental import pallas as pl
from jax.experimental.pallas import tpu as pltpu
from jax.sharding import PartitionSpec as P

EDGE = 8
HALO = 8
BF = jnp.bfloat16
F32 = jnp.float32


def dot(a, b):
    return lax.dot_general(a, b, (((1,), (0,)), ((), ())), preferred_element_type=F32)


def dot_t(a, b):
    return lax.dot_general(a, b, (((0,), (0,)), ((), ())), preferred_element_type=F32)


def rolled(x, by):
    return pltpu.roll(x, by % x.shape[0], 0)


def lanes(*parts):
    return jnp.concatenate(parts, axis=-1)


def blocks(rows):
    return jnp.concatenate([lanes(*row) for row in rows], axis=0)


def strided_block(w, r, z):
    return blocks([[w(r, 1), z], [w(r, 2), w(r, 0)]])


def spread_block(w, r, z):
    return blocks([[w(r, 1), w(r, 2)], [z, w(r, 0)]])


def paired_block(w, c, z):
    return blocks([[w(0, c), z], [w(1, c), w(0, c)], [w(2, c), w(1, c)], [z, w(2, c)]])


def flat(x):
    return x.reshape(x.shape[0] * x.shape[1], x.shape[2])


def compute(scale, raw_f, raw_c, rows_in, cols_in, corners, w_in, out, gout, grads,
            f, c, tmp, otmp, bd, bg, bm, bn, bu, bf, dp, gps, gpp, s1, s2, acc_u, acc_m, acc_d):
    half = raw_f.shape[0] // 2
    wd, wm, wu = w_in.at[0], w_in.at[1], w_in.at[2]
    wide = f.shape[2]
    ch = f.shape[3] // 2
    cols = wide - 2 * EDGE
    z = jnp.zeros((ch, ch), BF)
    lat = lax.axis_index("lat")
    first = lat == 0
    last = lat == lax.axis_size("lat") - 1
    low = jnp.where(first, 0, -(1 << 20))
    high = jnp.where(last, half, 1 << 20)

    def plain(ref):
        return lambda r, k: ref[r, k]

    def turned(ref):
        return lambda r, k: ref[r, k].T

    def flipped(ref):
        return lambda r, k: ref[2 - r, 2 - k].T

    for r in range(3):
        at = pl.ds(2 * ch * r, 2 * ch)
        bd[at, :] = strided_block(plain(wd), r, z)
        bg[at, :] = strided_block(turned(wu), r, z)
        bu[at, :] = spread_block(plain(wu), r, z)
        bf[at, :] = spread_block(turned(wd), r, z)
        bm[:, at] = paired_block(plain(wm), r, z)
        bn[:, at] = paired_block(flipped(wm), r, z)

    def inside(rows):
        return jnp.logical_and(rows >= low, rows < high)

    def row_mask(n, base, shape_cols):
        rows = base + lax.broadcasted_iota(jnp.int32, (n, wide, shape_cols), 0)
        return inside(rows)

    def pair_mask(n, base):
        shape = (n, wide, 2 * ch)
        rows = (base + 2 * lax.broadcasted_iota(jnp.int32, shape, 0)
                + (lax.broadcasted_iota(jnp.int32, shape, 2) >= ch).astype(jnp.int32))
        return inside(rows)

    def strided(src, start, n, weight):
        x0 = src[pl.ds(start, n), 1]
        x1 = src[pl.ds(start + 1, n), 0]
        x2 = src[pl.ds(start + 1, n), 1]
        acc = dot(flat(lanes(x0, x1, x2)), weight[...])
        return acc[:, :ch] + rolled(acc[:, ch:], 1)

    def to_pairs(x, n):
        x = x.reshape(n, 2, wide, ch)
        return lanes(x[:, 0], x[:, 1])

    def same(src, start, n, weight):
        acc = dot(flat(lanes(src[pl.ds(start, n)], src[pl.ds(start + 1, n)])), weight[...])
        k = 2 * ch
        total = rolled(acc[:, :k], 1) + acc[:, k:2 * k] + rolled(acc[:, 2 * k:], -1)
        return total

    side = jnp.zeros((8, HALO, ch), F32)
    full = 2 * cols
    tmp[:, 0:HALO, :] = side
    tmp[:, full + 3 * HALO:, :] = side

    def lay(dst, pair, middle, lower, upper):
        tmp[:, HALO:2 * HALO, :] = lower.astype(F32).reshape(8, HALO, ch)
        tmp[:, 2 * HALO:2 * HALO + full, :] = middle.astype(F32)
        tmp[:, 2 * HALO + full:3 * HALO + full, :] = upper.astype(F32).reshape(8, HALO, ch)
        even = tmp[:, pl.ds(0, wide, stride=2), :]
        odd = tmp[:, pl.ds(1, wide, stride=2), :]
        dst[pl.ds(pair, 4)] = lanes(even, odd).astype(BF).reshape(4, 2, wide, 2 * ch)

    for a, (dst, raw) in enumerate(((f, raw_f), (c, raw_c))):
        lay(dst, 0, rows_in[a, 0], corners[0, 0, a], corners[0, 1, a])
        lay(dst, half + 4, rows_in[a, 1], corners[1, 0, a], corners[1, 1, a])
        dst[half + 8] = jnp.zeros((2, wide, 2 * ch), BF)

        def lay_step(t, _, a=a, dst=dst, raw=raw):
            lay(dst, 4 * t + 4, raw[pl.ds(8 * t, 8)], cols_in[0, a, pl.ds(4 * t, 4)],
                cols_in[1, a, pl.ds(4 * t, 4)])
            return 0

        lax.fori_loop(0, half // 4, lay_step, 0)

    pairs = (half + 8) // 2
    nd = 6 if pairs % 6 == 0 else 1

    def down_step(t, _):
        q = t * nd
        v = strided(f, 2 * q, 2 * nd, bd)
        v = to_pairs(v, nd)
        dp[pl.ds(q, nd)] = jnp.where(pair_mask(nd, 2 * q - 3), v, 0.0).astype(BF)
        return 0

    lax.fori_loop(0, pairs // nd, down_step, 0)

    def shifted_rows(dst, start, n, v):
        nxt = rolled(v, -1)
        for a in range(2):
            half_lanes = slice(a * ch, (a + 1) * ch)
            piece = lanes(v[:, half_lanes], nxt[:, half_lanes]).astype(BF)
            dst[pl.ds(start, n), a] = piece.reshape(n, wide, 2 * ch)

    pairs_mid = (half + 4) // 2
    nm = 11 if pairs_mid % 11 == 0 else 1

    def mid_step(t, _):
        p = t * nm
        pre = same(dp, p, nm, bm)
        g = strided(c, 2 * p + 1, 2 * nm, bg)
        g = flat(to_pairs(g, nm))
        sig = jax.nn.sigmoid(pre)
        ok = flat(pair_mask(nm, 2 * p - 2))
        mid = jnp.where(ok, pre * sig, 0.0)
        gp = jnp.where(ok, g * sig * (1.0 + pre * (1.0 - sig)), 0.0)
        shifted_rows(s1, p, nm, mid)
        gpp[pl.ds(p, nm)] = gp.astype(BF).reshape(nm, wide, 2 * ch)
        place = lax.broadcasted_iota(jnp.int32, (nm, wide, 2 * ch), 1)
        own = flat(jnp.logical_and(place >= EDGE, place < EDGE + cols))
        gm = jnp.where(own, gp, 0.0)
        after, before = rolled(gm, -1), rolled(gm, 1)
        for a in range(2):
            k = slice(a * ch, (a + 1) * ch)
            piece = lanes(after[:, k], gm[:, k], before[:, k]).astype(BF)
            gps[pl.ds(p, nm), a] = piece.reshape(nm, wide, 3 * ch)
        return 0

    lax.fori_loop(0, pairs_mid // nm, mid_step, 0)

    pairs_gd = (half + 2) // 2
    ng = 7 if pairs_gd % 7 == 0 else 1

    def gd_step(t, _):
        q = t * ng
        v = same(gpp, q, ng, bn)
        v = jnp.where(flat(pair_mask(ng, 2 * q - 1)), v, 0.0)
        shifted_rows(s2, q, ng, v)
        return 0

    lax.fori_loop(0, pairs_gd // ng, gd_step, 0)

    acc_u[...] = jnp.zeros_like(acc_u)
    acc_m[...] = jnp.zeros_like(acc_m)
    acc_d[...] = jnp.zeros_like(acc_d)
    place = lax.broadcasted_iota(jnp.int32, (wide, 2 * ch), 0)
    place = place + (lax.broadcasted_iota(jnp.int32, (wide, 2 * ch), 1) >= ch).astype(jnp.int32)
    own = jnp.logical_and(place >= EDGE, place < EDGE + cols).astype(F32).astype(BF)[None]
    step = 4

    def taps(src, i, n):
        return flat(lanes(src[pl.ds(i + 3, n), 1], src[pl.ds(i + 4, n), 0], src[pl.ds(i + 4, n), 1]))

    def grads_step(t, _):
        p = t * step
        n = 2 * step
        i = 2 * p
        m = s1[pl.ds(p + 1, step)].reshape(n, wide, 2 * ch) * own
        acc_u[...] += dot_t(flat(m), taps(c, i, n))
        ga = s2[pl.ds(p, step + 1)].reshape(2 * step + 2, wide, 2 * ch)[1:1 + n] * own
        acc_d[...] += dot_t(flat(ga), taps(f, i, n))
        d0, d1 = dp[pl.ds(p + 1, step)], dp[pl.ds(p + 2, step)]
        acc_m[...] += (
            dot_t(flat(gps[pl.ds(p + 1, step), 0]), flat(lanes(d0, d1[:, :, :ch])))
            + dot_t(flat(gps[pl.ds(p + 1, step), 1]), flat(lanes(d0[:, :, ch:], d1)))
        )
        return 0

    lax.fori_loop(0, half // (2 * step), grads_step, 0)

    part = ch // 2

    def put(tap, value):
        value = value.astype(BF)
        for h in range(2):
            grads[h, tap * part:(tap + 1) * part, :] = value[h * part:(h + 1) * part]

    for r in range(3):
        for k in range(3):
            top = ch if k == 0 else 0
            left = 2 * ch * r + (0 if k == 1 else ch)
            tap = 3 * r + k
            put(tap, (acc_d[top:top + ch, left:left + ch] * scale).T)
            put(9 + tap, (acc_m[k * ch:(k + 1) * ch, r * ch:(r + 1) * ch] * scale).T)
            put(18 + tap, acc_u[top:top + ch, left:left + ch] * scale)
    rest = grads.shape[1] - 27 * part
    if rest:
        grads[:, 27 * part:, :] = jnp.zeros((2, rest, ch), BF)

    def up_step(t, _):
        i = t * n_up
        def rows1(at, n):
            q = t * (n_up // 2) + 1
            return s1[pl.ds(q, n // 2 + 1)].reshape(n + 2, wide, 2 * ch)[at:at + n]
        def rows2(at, n):
            q = t * (n_up // 2)
            return s2[pl.ds(q, n // 2 + 1)].reshape(n + 2, wide, 2 * ch)[at + 1:at + 1 + n]
        for rows, base, dst, weight in ((rows1, raw_f, out, bu), (rows2, raw_c, gout, bf)):
            lo, hi = flat(rows(0, n_up)), flat(rows(1, n_up))
            k = 2 * ch
            even = dot(lo, weight[k:2 * k, :])
            odd = dot(lo, weight[2 * k:, :]) + dot(hi, weight[:k, :])
            for a, v in enumerate((even, odd)):
                v = v.reshape(n_up, wide, k)[:, EDGE:EDGE + cols]
                otmp[:, a, pl.ds(0, cols, stride=2), :] = v[:, :, :ch]
                otmp[:, a, pl.ds(1, cols, stride=2), :] = v[:, :, ch:]
            at = pl.ds(2 * i, 2 * n_up)
            total = base[at].astype(F32) + otmp[...].reshape(2 * n_up, full, ch)
            dst[at] = total.astype(BF)
        return 0

    n_up = 8
    lax.fori_loop(0, half // n_up, up_step, 0)


def exchange(f, c, wd, wm, wu, rows_out, cols_out, corners, w_out, packed, send, recv):
    rows, full, ch = f.shape
    lat, lon, core = (lax.axis_index(name) for name in ("lat", "lon", "dp"))
    n_lat, n_lon = lax.axis_size("lat"), lax.axis_size("lon")
    below, above = lat > 0, lat < n_lat - 1
    west, east = lax.rem(lon + n_lon - 1, n_lon), lax.rem(lon + 1, n_lon)
    other = 1 - core
    barrier = pltpu.get_barrier_semaphore()

    def greet(**where):
        pl.semaphore_signal(barrier, inc=1, device_id=where, device_id_type=pl.DeviceIdType.MESH)

    greet(lon=west)
    greet(lon=east)
    greet(dp=other)
    for ok, to in ((below, lat - 1), (above, lat + 1)):
        @pl.when(ok)
        def _():
            greet(lat=to)
            greet(lat=to, lon=west)
            greet(lat=to, lon=east)

    for a, src in enumerate((f, c)):
        for d, start in ((0, full - 16), (1, 0)):
            x = src[:, start:start + 16, :].astype(F32)
            x = x[:, 8:] if d == 0 else x[:, :8]
            packed[d, a] = x.reshape(rows // 2, 16, ch).astype(BF)
    part = wd.shape[2]
    mine = pl.ds(pl.multiple_of(core * part, part), part)
    for k, w in enumerate((wd, wm, wu)):
        w_out[k, :, :, mine, :] = w[...]
    for d, ok in ((0, below), (1, above)):
        @pl.when(jnp.logical_not(ok))
        def _():
            rows_out[:, d] = jnp.zeros_like(rows_out[:, d])
            corners[d] = jnp.zeros_like(corners[d])

    pl.semaphore_wait(barrier, 3 + 3 * below.astype(jnp.int32) + 3 * above.astype(jnp.int32))

    copies = []

    def remote(src, dst, sends, gets, **where):
        i = len(copies)
        copies.append((pltpu.make_async_remote_copy(
            src_ref=src, dst_ref=dst, send_sem=send.at[i], recv_sem=recv.at[i],
            device_id=where, device_id_type=pl.DeviceIdType.MESH), sends, gets))

    for d, to in ((0, east), (1, west)):
        remote(packed.at[d], cols_out.at[d], None, None, lon=to)
    for d, to, sends, gets in ((0, lat + 1, above, below), (1, lat - 1, below, above)):
        begin = rows - 8 if d == 0 else 0
        for a, src in enumerate((f, c)):
            remote(src.at[pl.ds(begin, 8)], rows_out.at[a, d], sends, gets, lat=to)
        for e, side in ((0, east), (1, west)):
            remote(packed.at[e, :, pl.ds(begin // 2, 4)], corners.at[d, e], sends, gets, lat=to, lon=side)
    for k, w in enumerate((wd, wm, wu)):
        remote(w, w_out.at[k, :, :, mine, :], None, None, dp=other)

    def under(condition, act):
        if condition is None:
            act()
        else:
            pl.when(condition)(act)

    for copy, sends, _ in copies:
        under(sends, copy.start)
    for copy, sends, gets in copies:
        under(sends, copy.wait_send)
        under(gets, copy.wait_recv)


def reduce(g, down, mid, up, got, st1, acc1, r2, st2, acc2, r3, whole, send, recv):
    lat, lon, core = (lax.axis_index(name) for name in ("lat", "lon", "dp"))
    n_lat, n_lon = lax.axis_size("lat"), lax.axis_size("lon")
    other = 1 - core
    share, piece = r2.shape[1], r3.shape[1]
    east = [lax.rem(lon + k, n_lon) for k in range(1, n_lon)]
    north = [lax.rem(lat + k, n_lat) for k in range(1, n_lat)]
    barrier = pltpu.get_barrier_semaphore()
    peers = [dict(dp=other)] + [dict(lon=p) for p in east] + [dict(lat=p) for p in north]
    for where in peers:
        pl.semaphore_signal(barrier, inc=1, device_id=where, device_id_type=pl.DeviceIdType.MESH)
    pl.semaphore_wait(barrier, len(peers))
    used = [0]

    def remote(src, dst, **where):
        i = used[0]
        used[0] += 1
        copy = pltpu.make_async_remote_copy(
            src_ref=src, dst_ref=dst, send_sem=send.at[i], recv_sem=recv.at[i],
            device_id=where, device_id_type=pl.DeviceIdType.MESH)
        copy.start()
        return copy

    def at(index, size):
        return pl.ds(pl.multiple_of(index * size, 16), size)

    remote(g.at[other], got, dp=other).wait()
    total = g[core].astype(F32) + got[...].astype(F32)
    acc1[...] = total
    st1[...] = total.astype(BF)
    copies = [remote(st1.at[at(p, share)], r2.at[k], lon=p) for k, p in enumerate(east)]
    for copy in copies:
        copy.wait()
    total = acc1[at(lon, share)]
    for k in range(n_lon - 1):
        total = total + r2[k].astype(F32)
    acc2[...] = total
    st2[...] = total.astype(BF)
    copies = [remote(st2.at[at(p, piece)], r3.at[k], lat=p) for k, p in enumerate(north)]
    for copy in copies:
        copy.wait()
    total = acc2[at(lat, piece)]
    for k in range(n_lat - 1):
        total = total + r3[k].astype(F32)
    own = pl.ds(pl.multiple_of(lon * share + lat * piece, 16), piece)
    whole[own] = total.astype(BF)
    copies = [remote(whole.at[own], whole.at[own], lat=p) for p in north]
    for copy in copies:
        copy.wait()
    band = at(lon, share)
    copies = [remote(whole.at[band], whole.at[band], lon=p) for p in east]
    for copy in copies:
        copy.wait()
    n = down.shape[0]
    for k, dst in enumerate((down, mid, up)):
        dst[...] = whole[k * n:(k + 1) * n].astype(F32)


def body(fields, down_weight, mid_weight, up_weight, cotangent):
    _, rows, full, ch = fields.shape
    half, cols = rows // 2, full // 2
    wide = cols + 2 * EDGE
    n_lat, n_lon = lax.axis_size("lat"), lax.axis_size("lon")
    cells = lax.axis_size("dp") * rows * n_lat * full * n_lon
    scale = 1.0 / math.sqrt(cells)
    k = 2 * ch
    vm = pl.BlockSpec(memory_space=pltpu.VMEM)

    def sds(shape, dtype=BF):
        return jax.ShapeDtypeStruct(shape, dtype)

    f, c = fields[0], cotangent[0]
    halo = pl.pallas_call(
        exchange,
        out_shape=(
            sds((2, 2, 8, full, ch)),
            sds((2, 2, half, 16, ch)),
            sds((2, 2, 2, 4, 16, ch)),
            sds((3, 3, 3, ch, ch)),
        ),
        in_specs=[vm] * 5,
        out_specs=(vm,) * 4,
        scratch_shapes=[
            pltpu.VMEM((2, 2, half, 16, ch), BF),
            pltpu.SemaphoreType.DMA((13,)),
            pltpu.SemaphoreType.DMA((13,)),
        ],
        compiler_params=pltpu.CompilerParams(
            collective_id=0, has_side_effects=True, vmem_limit_bytes=40 << 20),
    )(f, c, down_weight, mid_weight, up_weight)

    unit = n_lat * n_lon * 16
    taps = 27 * (ch // 2)
    padded = -(-taps // unit) * unit
    out, gout, grads = pl.pallas_call(
        functools.partial(compute, scale),
        out_shape=(sds((rows, full, ch)), sds((rows, full, ch)), sds((2, padded, ch))),
        in_specs=[vm] * 6,
        out_specs=(vm, vm, vm),
        scratch_shapes=[
            pltpu.VMEM((half + 9, 2, wide, k), BF),
            pltpu.VMEM((half + 9, 2, wide, k), BF),
            pltpu.VMEM((8, full + 4 * HALO, ch), F32),
            pltpu.VMEM((8, 2, full, ch), F32),
            pltpu.VMEM((3 * k, k), BF),
            pltpu.VMEM((3 * k, k), BF),
            pltpu.VMEM((2 * k, 3 * k), BF),
            pltpu.VMEM((2 * k, 3 * k), BF),
            pltpu.VMEM((3 * k, k), BF),
            pltpu.VMEM((3 * k, k), BF),
            pltpu.VMEM(((half + 8) // 2, wide, k), BF),
            pltpu.VMEM(((half + 4) // 2, 2, wide, 3 * ch), BF),
            pltpu.VMEM(((half + 4) // 2, wide, k), BF),
            pltpu.VMEM(((half + 4) // 2, 2, wide, k), BF),
            pltpu.VMEM(((half + 2) // 2, 2, wide, k), BF),
            pltpu.VMEM((k, 3 * k), F32),
            pltpu.VMEM((3 * ch, 3 * ch), F32),
            pltpu.VMEM((k, 3 * k), F32),
        ],
        compiler_params=pltpu.CompilerParams(vmem_limit_bytes=56 << 20),
    )(f, c, *halo)

    share, piece = padded // n_lon, padded // (n_lon * n_lat)
    count = 1 + 2 * (n_lon - 1) + 2 * (n_lat - 1)
    terms = pl.pallas_call(
        reduce,
        out_shape=(sds((taps // 3, ch), F32),) * 3,
        in_specs=[vm],
        out_specs=(vm,) * 3,
        scratch_shapes=[
            pltpu.VMEM((padded, ch), BF),
            pltpu.VMEM((padded, ch), BF),
            pltpu.VMEM((padded, ch), F32),
            pltpu.VMEM((n_lon - 1, share, ch), BF),
            pltpu.VMEM((share, ch), BF),
            pltpu.VMEM((share, ch), F32),
            pltpu.VMEM((n_lat - 1, piece, ch), BF),
            pltpu.VMEM((padded, ch), BF),
            pltpu.SemaphoreType.DMA((count,)),
            pltpu.SemaphoreType.DMA((count,)),
        ],
        compiler_params=pltpu.CompilerParams(
            collective_id=1, has_side_effects=True, vmem_limit_bytes=40 << 20),
    )(grads)
    return (out[None], gout[None]) + tuple(t.reshape(3, 3, ch // 2, ch) for t in terms)


def solution(mesh):
    maps = P("dp", "lat", "lon", None)
    kernel = P(None, None, "dp", None)
    return jax.shard_map(
        body,
        mesh=mesh,
        in_specs=(maps, kernel, kernel, kernel, maps),
        out_specs=(maps, maps, kernel, kernel, kernel),
        check_vma=False,
    )
```

```python
import functools
import math

import jax
import jax.numpy as jnp
from jax import lax
from jax.experimental import pallas as pl
from jax.experimental.pallas import tpu as pltpu
from jax.sharding import PartitionSpec as P

EDGE = 8
HALO = 8
BF = jnp.bfloat16
F32 = jnp.float32


def dot(a, b):
    return lax.dot_general(a, b, (((1,), (0,)), ((), ())), preferred_element_type=F32)


def dot_t(a, b):
    return lax.dot_general(a, b, (((0,), (0,)), ((), ())), preferred_element_type=F32)


def rolled(x, by):
    return pltpu.roll(x, by % x.shape[0], 0)


def lanes(*parts):
    return jnp.concatenate(parts, axis=-1)


def blocks(rows):
    return jnp.concatenate([lanes(*row) for row in rows], axis=0)


def strided_block(w, r, z):
    return blocks([[w(r, 1), z], [w(r, 2), w(r, 0)]])


def spread_block(w, r, z):
    return blocks([[w(r, 1), w(r, 2)], [z, w(r, 0)]])


def paired_block(w, c, z):
    return blocks([[w(0, c), z], [w(1, c), w(0, c)], [w(2, c), w(1, c)], [z, w(2, c)]])


def flat(x):
    return x.reshape(x.shape[0] * x.shape[1], x.shape[2])


def level(scale, f_in, c_in, wd_in, wm_in, wu_in, out, gout, down_out, mid_out, up_out,
          raw_f, raw_c, rows_in, low_in, high_in, pair_in, low_at, high_at, pair_at,
          low_out, high_out, pair_out, w_in, local, send, recv,
          f, c, tmp, otmp, bd, bg, bm, bn, bu, bf, dp, gps, gpp, s1, s2, acc_u, acc_m, acc_d,
          *sums):
    rows = raw_f.shape[0]
    half = rows // 2
    wd, wm, wu = w_in.at[0], w_in.at[1], w_in.at[2]
    wide = f.shape[2]
    ch = f.shape[3] // 2
    cols = wide - 2 * EDGE
    z = jnp.zeros((ch, ch), BF)
    lat = lax.axis_index("lat")
    lon, core = lax.axis_index("lon"), lax.axis_index("dp")
    n_lat, n_lon = lax.axis_size("lat"), lax.axis_size("lon")
    other = 1 - core
    below, above = lat > 0, lat < n_lat - 1
    low = jnp.where(below, -(1 << 20), 0)
    high = jnp.where(above, 1 << 20, half)
    full = 2 * cols
    east = [lax.rem(lon + k, n_lon) for k in range(1, n_lon)]
    north = [lax.rem(lat + k, n_lat) for k in range(1, n_lat)]

    rows_in[...] = jnp.zeros_like(rows_in)
    for ref in (low_at, high_at, pair_at):
        ref[...] = jnp.zeros_like(ref)

    barrier = pltpu.get_barrier_semaphore()

    def greet(**where):
        pl.semaphore_signal(barrier, inc=1, device_id=where, device_id_type=pl.DeviceIdType.MESH)

    greet(dp=other)
    for p in east:
        greet(lon=p)
    for p in north:
        greet(lat=p)
    for ok, to in ((below, lat - 1), (above, lat + 1)):
        @pl.when(ok)
        def _(to=to):
            greet(lat=to, lon=east[0])
            greet(lat=to, lon=east[-1])

    part = ch // 2
    mine = pl.ds(pl.multiple_of(core * part, part), part)
    loads = [pltpu.make_async_copy(f_in, raw_f, local.at[0]), pltpu.make_async_copy(c_in, raw_c, local.at[1])]
    for i, w in enumerate((wd_in, wm_in, wu_in)):
        loads.append(pltpu.make_async_copy(w, w_in.at[i, :, :, mine, :], local.at[2 + i]))
    for load in loads:
        load.start()
    pl.semaphore_wait(barrier, n_lon + n_lat - 1 + 2 * below.astype(jnp.int32) + 2 * above.astype(jnp.int32))

    used = [0]

    def remote(src, dst, **where):
        i = used[0]
        used[0] += 1
        return pltpu.make_async_remote_copy(
            src_ref=src, dst_ref=dst, send_sem=send.at[i], recv_sem=recv.at[i],
            device_id=where, device_id_type=pl.DeviceIdType.MESH)

    def under(condition, act):
        if condition is None:
            act()
        else:
            pl.when(condition)(act)

    halos = []
    for k, w in enumerate((wd_in, wm_in, wu_in)):
        halos.append((remote(w, w_in.at[k, :, :, mine, :], dp=other), None, None))
    for a, src in enumerate((f_in, c_in)):
        n0, n1 = (5, 6) if a == 0 else (3, 4)
        halos.append((remote(src.at[pl.ds(rows - n0, n0)], rows_in.at[a, 0, pl.ds(8 - n0, n0)], lat=lat + 1), above, below))
        halos.append((remote(src.at[pl.ds(0, n1)], rows_in.at[a, 1, pl.ds(0, n1)], lat=lat - 1), below, above))
    early = len(halos)
    for copy, sends, _ in halos:
        under(sends, copy.start)

    loads[0].wait()
    loads[1].wait()

    def slots(n):
        return lax.broadcasted_iota(jnp.int32, (n, HALO, ch), 1)

    x_f = raw_f[:, full - 16:, :].astype(F32)[:, 8:]
    x_c = raw_c[:, full - 16:, :].astype(F32)[:, 8:]
    x = jnp.where(slots(rows) < 5, pltpu.roll(x_f, 5, 1), x_c)
    low_out[...] = x.reshape(half, 16, ch).astype(BF)
    high_out[...] = raw_f[:, :16, :].astype(F32)[:, :8].reshape(half, 16, ch).astype(BF)
    x = raw_c[:, :16, :].astype(F32)[:, :8].reshape(half, 2, HALO, ch)
    x = jnp.where(slots(half) < 4, x[:, 0], pltpu.roll(x[:, 1], 4, 1))
    pair_out[...] = x.reshape(half // 2, 16, ch).astype(BF)

    halos.append((remote(low_out, low_in, lon=east[0]), None, None))
    halos.append((remote(high_out, high_in, lon=east[-1]), None, None))
    halos.append((remote(pair_out, pair_in, lon=east[-1]), None, None))
    for d, to, sends, gets in ((0, lat + 1, above, below), (1, lat - 1, below, above)):
        begin = half - 4 if d == 0 else 0
        here = pl.ds(begin, 4)
        halos.append((remote(low_out.at[here], low_at.at[d], lat=to, lon=east[0]), sends, gets))
        halos.append((remote(high_out.at[here], high_at.at[d], lat=to, lon=east[-1]), sends, gets))
        here = pl.ds(begin // 2, 2)
        halos.append((remote(pair_out.at[here], pair_at.at[d], lat=to, lon=east[-1]), sends, gets))
    for copy, sends, _ in halos[early:]:
        under(sends, copy.start)
    for load in loads[2:]:
        load.wait()

    def landed(part_of):
        for copy, sends, gets in part_of:
            under(sends, copy.wait_send)
            under(gets, copy.wait_recv)

    def plain(ref):
        return lambda r, k: ref[r, k]

    def turned(ref):
        return lambda r, k: ref[r, k].T

    def flipped(ref):
        return lambda r, k: ref[2 - r, 2 - k].T

    def inside(at):
        return jnp.logical_and(at >= low, at < high)

    def pair_mask(n, base):
        shape = (n, wide, 2 * ch)
        rows = (base + 2 * lax.broadcasted_iota(jnp.int32, shape, 0)
                + (lax.broadcasted_iota(jnp.int32, shape, 2) >= ch).astype(jnp.int32))
        return inside(rows)

    def strided(src, start, n, weight):
        x0 = src[pl.ds(start, n), 1]
        x1 = src[pl.ds(start + 1, n), 0]
        x2 = src[pl.ds(start + 1, n), 1]
        acc = dot(flat(lanes(x0, x1, x2)), weight[...])
        return acc[:, :ch] + rolled(acc[:, ch:], 1)

    def to_pairs(x, n):
        x = x.reshape(n, 2, wide, ch)
        return lanes(x[:, 0], x[:, 1])

    def same(src, start, n, weight):
        acc = dot(flat(lanes(src[pl.ds(start, n)], src[pl.ds(start + 1, n)])), weight[...])
        k = 2 * ch
        total = rolled(acc[:, :k], 1) + acc[:, k:2 * k] + rolled(acc[:, 2 * k:], -1)
        return total

    side = jnp.zeros((8, 2 * HALO, ch), F32)
    tmp[:, 0:2 * HALO, :] = side
    tmp[:, full + 2 * HALO:, :] = side

    def lay(dst, pair, middle):
        tmp[:, 2 * HALO:2 * HALO + full, :] = middle.astype(F32)
        even = tmp[:, pl.ds(0, wide, stride=2), :]
        odd = tmp[:, pl.ds(1, wide, stride=2), :]
        dst[pl.ds(pair, 4)] = lanes(even, odd).astype(BF).reshape(4, 2, wide, 2 * ch)

    def lay_step(t, _):
        lay(f, 4 * t + 4, raw_f[pl.ds(8 * t, 8)])
        lay(c, 4 * t + 4, raw_c[pl.ds(8 * t, 8)])
        return 0

    lax.fori_loop(0, half // 4, lay_step, 0)
    for dst in (f, c):
        dst[half + 8] = jnp.zeros((2, wide, 2 * ch), BF)

    landed(halos[:3])
    for r in range(3):
        at = pl.ds(2 * ch * r, 2 * ch)
        bd[at, :] = strided_block(plain(wd), r, z)
        bg[at, :] = strided_block(turned(wu), r, z)
        bu[at, :] = spread_block(plain(wu), r, z)
        bf[at, :] = spread_block(turned(wd), r, z)
        bm[:, at] = paired_block(plain(wm), r, z)
        bn[:, at] = paired_block(flipped(wm), r, z)

    landed(halos[3:early])
    for a, dst in enumerate((f, c)):
        lay(dst, 0, rows_in[a, 0])
        lay(dst, half + 4, rows_in[a, 1])

    landed(halos[early:])

    def edge(dst, pair, lower, upper):
        tmp[:, HALO:2 * HALO, :] = lower
        tmp[:, 3 * HALO:4 * HALO, :] = jnp.zeros_like(lower)
        tmp[:, 2 * HALO:3 * HALO, :] = upper
        at = pl.ds(pair, 4)
        new = lanes(tmp[:, pl.ds(0, HALO, stride=2), :], tmp[:, pl.ds(1, HALO, stride=2), :])
        old = dst[at, :, 0:16, :].astype(F32).reshape(8, 16, 2 * ch)
        dst[at, :, 0:16, :] = jnp.concatenate([new, old[:, 8:]], axis=1).astype(BF).reshape(4, 2, 16, 2 * ch)
        new = lanes(tmp[:, pl.ds(2 * HALO, HALO, stride=2), :], tmp[:, pl.ds(2 * HALO + 1, HALO, stride=2), :])
        old = dst[at, :, wide - 16:, :].astype(F32).reshape(8, 16, 2 * ch)
        dst[at, :, wide - 16:, :] = jnp.concatenate([old[:, :8], new], axis=1).astype(BF).reshape(4, 2, 16, 2 * ch)

    def edges(pair, lower, upper, paired):
        slot = slots(8)
        z8 = jnp.zeros((8, HALO, ch), F32)
        lower = lower.astype(F32).reshape(8, HALO, ch)
        upper = upper.astype(F32).reshape(8, HALO, ch)
        paired = paired.astype(F32).reshape(4, 1, HALO, ch)
        paired = jnp.concatenate([paired, pltpu.roll(paired.reshape(4, HALO, ch), 4, 1)[:, None]], axis=1)
        paired = paired.reshape(8, HALO, ch)
        edge(f, pair, jnp.where(slot >= 3, pltpu.roll(lower, 3, 1), z8), upper)
        edge(c, pair, jnp.where(slot >= 5, lower, z8), jnp.where(slot < 4, paired, z8))

    tmp[:, 0:HALO, :] = jnp.zeros((8, HALO, ch), F32)

    def edge_step(t, _):
        at = pl.ds(4 * t, 4)
        edges(4 * t + 4, low_in[at], high_in[at], pair_in[pl.ds(2 * t, 2)])
        return 0

    lax.fori_loop(0, half // 4, edge_step, 0)
    edges(0, low_at[0], high_at[0], pair_at[0])
    edges(half + 4, low_at[1], high_at[1], pair_at[1])

    pairs = (half + 8) // 2
    nd = 6 if pairs % 6 == 0 else 1

    def down_step(t, _):
        q = t * nd
        v = strided(f, 2 * q, 2 * nd, bd)
        v = to_pairs(v, nd)
        dp[pl.ds(q, nd)] = jnp.where(pair_mask(nd, 2 * q - 3), v, 0.0).astype(BF)
        return 0

    lax.fori_loop(0, pairs // nd, down_step, 0)

    def shifted_rows(dst, start, n, v):
        nxt = rolled(v, -1)
        for a in range(2):
            half_lanes = slice(a * ch, (a + 1) * ch)
            piece = lanes(v[:, half_lanes], nxt[:, half_lanes]).astype(BF)
            dst[pl.ds(start, n), a] = piece.reshape(n, wide, 2 * ch)

    pairs_mid = (half + 4) // 2
    nm = 11 if pairs_mid % 11 == 0 else 1

    def mid_step(t, _):
        p = t * nm
        pre = same(dp, p, nm, bm)
        g = strided(c, 2 * p + 1, 2 * nm, bg)
        g = flat(to_pairs(g, nm))
        sig = jax.nn.sigmoid(pre)
        ok = flat(pair_mask(nm, 2 * p - 2))
        mid = jnp.where(ok, pre * sig, 0.0)
        gp = jnp.where(ok, g * sig * (1.0 + pre * (1.0 - sig)), 0.0)
        shifted_rows(s1, p, nm, mid)
        gpp[pl.ds(p, nm)] = gp.astype(BF).reshape(nm, wide, 2 * ch)
        place = lax.broadcasted_iota(jnp.int32, (nm, wide, 2 * ch), 1)
        own = flat(jnp.logical_and(place >= EDGE, place < EDGE + cols))
        gm = jnp.where(own, gp, 0.0)
        after, before = rolled(gm, -1), rolled(gm, 1)
        for a in range(2):
            k = slice(a * ch, (a + 1) * ch)
            piece = lanes(after[:, k], gm[:, k], before[:, k]).astype(BF)
            gps[pl.ds(p, nm), a] = piece.reshape(nm, wide, 3 * ch)
        return 0

    lax.fori_loop(0, pairs_mid // nm, mid_step, 0)

    acc_u[...] = jnp.zeros_like(acc_u)
    acc_m[...] = jnp.zeros_like(acc_m)
    acc_d[...] = jnp.zeros_like(acc_d)
    place = lax.broadcasted_iota(jnp.int32, (wide, 2 * ch), 0)
    place = place + (lax.broadcasted_iota(jnp.int32, (wide, 2 * ch), 1) >= ch).astype(jnp.int32)
    own = jnp.logical_and(place >= EDGE, place < EDGE + cols).astype(F32).astype(BF)[None]
    step = 4

    def taps(src, i, n):
        return flat(lanes(src[pl.ds(i + 3, n), 1], src[pl.ds(i + 4, n), 0], src[pl.ds(i + 4, n), 1]))

    def first_grads(t, _):
        p = t * step
        n = 2 * step
        m = s1[pl.ds(p + 1, step)].reshape(n, wide, 2 * ch) * own
        acc_u[...] += dot_t(flat(m), taps(c, 2 * p, n))
        d0, d1 = dp[pl.ds(p + 1, step)], dp[pl.ds(p + 2, step)]
        acc_m[...] += (
            dot_t(flat(gps[pl.ds(p + 1, step), 0]), flat(lanes(d0, d1[:, :, :ch])))
            + dot_t(flat(gps[pl.ds(p + 1, step), 1]), flat(lanes(d0[:, :, ch:], d1)))
        )
        return 0

    def last_grads(t, _):
        p = t * step
        n = 2 * step
        ga = s2[pl.ds(p, step + 1)].reshape(2 * step + 2, wide, 2 * ch)[1:1 + n] * own
        acc_d[...] += dot_t(flat(ga), taps(f, 2 * p, n))
        return 0

    def put(grads, tap, value):
        value = value.astype(BF)
        for h in range(2):
            grads[h, tap * part:(tap + 1) * part, :] = value[h * part:(h + 1) * part]

    def clear(grads, count):
        rest = grads.shape[1] - count * part
        if rest:
            grads[:, count * part:, :] = jnp.zeros((2, rest, ch), BF)

    batch_a = total_of(remote, sums[:8], (mid_out, up_out), lat, lon, core, north, east)
    batch_b = total_of(remote, sums[8:], (down_out,), lat, lon, core, north, east)

    lax.fori_loop(0, half // (2 * step), first_grads, 0)
    where = [(r, k, ch if k == 0 else 0, 2 * ch * r + (0 if k == 1 else ch)) for r in range(3) for k in range(3)]
    for r, k, top, left in where:
        tap = 3 * r + k
        put(sums[0], tap, (acc_m[k * ch:(k + 1) * ch, r * ch:(r + 1) * ch] * scale).T)
        put(sums[0], 9 + tap, acc_u[top:top + ch, left:left + ch] * scale)
    clear(sums[0], 18)
    next(batch_a)

    pairs_gd = (half + 2) // 2
    ng = 7 if pairs_gd % 7 == 0 else 1

    def gd_step(t, _):
        q = t * ng
        v = same(gpp, q, ng, bn)
        v = jnp.where(flat(pair_mask(ng, 2 * q - 1)), v, 0.0)
        shifted_rows(s2, q, ng, v)
        return 0

    lax.fori_loop(0, 1, gd_step, 0)
    next(batch_a)
    lax.fori_loop(1, pairs_gd // ng, gd_step, 0)
    lax.fori_loop(0, half // (2 * step), last_grads, 0)
    for r, k, top, left in where:
        put(sums[8], 3 * r + k, (acc_d[top:top + ch, left:left + ch] * scale).T)
    clear(sums[8], 9)
    next(batch_b)
    next(batch_a)

    def up_step(t, _):
        i = t * n_up
        def rows1(at, n):
            q = t * (n_up // 2) + 1
            return s1[pl.ds(q, n // 2 + 1)].reshape(n + 2, wide, 2 * ch)[at:at + n]
        def rows2(at, n):
            q = t * (n_up // 2)
            return s2[pl.ds(q, n // 2 + 1)].reshape(n + 2, wide, 2 * ch)[at + 1:at + 1 + n]
        for rows, base, dst, weight in ((rows1, raw_f, out, bu), (rows2, raw_c, gout, bf)):
            lo, hi = flat(rows(0, n_up)), flat(rows(1, n_up))
            k = 2 * ch
            even = dot(lo, weight[k:2 * k, :])
            odd = dot(lo, weight[2 * k:, :]) + dot(hi, weight[:k, :])
            for a, v in enumerate((even, odd)):
                v = v.reshape(n_up, wide, k)[:, EDGE:EDGE + cols]
                otmp[:, a, pl.ds(0, cols, stride=2), :] = v[:, :, :ch]
                otmp[:, a, pl.ds(1, cols, stride=2), :] = v[:, :, ch:]
            at = pl.ds(2 * i, 2 * n_up)
            total = base[at].astype(F32) + otmp[...].reshape(2 * n_up, full, ch)
            dst[at] = total.astype(BF)
        return 0

    n_up = 8
    steps = half // n_up
    cuts = [steps * i // 5 for i in range(6)]
    for i in range(5):
        lax.fori_loop(cuts[i], cuts[i + 1], up_step, 0)
        next(batch_b, None)
        next(batch_a, None)


def total_of(remote, refs, outs, lat, lon, core, north, east):
    g, got, st1, r2, st2, r3, whole, acc = refs
    share, piece = st2.shape[0], r3.shape[1]

    def at(index, size):
        return pl.ds(pl.multiple_of(index * size, 16), size)

    def begin(copies):
        for copy in copies:
            copy.start()
        return copies

    def end(copies):
        for copy in copies:
            copy.wait()

    copies = begin([remote(g.at[1 - core], got, dp=1 - core)])
    yield
    end(copies)
    total = g[core].astype(F32) + got[...].astype(F32)
    acc[...] = total
    st1[...] = total.astype(BF)
    copies = begin([remote(st1.at[at(p, share)], r2.at[k], lon=p) for k, p in enumerate(east)])
    yield
    end(copies)
    total = acc[at(lon, share)]
    for k in range(len(east)):
        total = total + r2[k].astype(F32)
    acc[0:share] = total
    st2[...] = total.astype(BF)
    copies = begin([remote(st2.at[at(p, piece)], r3.at[k], lat=p) for k, p in enumerate(north)])
    yield
    end(copies)
    total = acc[at(lat, piece)]
    for k in range(len(north)):
        total = total + r3[k].astype(F32)
    own = pl.ds(pl.multiple_of(lon * share + lat * piece, 16), piece)
    whole[own] = total.astype(BF)
    copies = begin([remote(whole.at[own], whole.at[own], lat=p) for p in north])
    yield
    end(copies)
    band = at(lon, share)
    copies = begin([remote(whole.at[band], whole.at[band], lon=p) for p in east])
    yield
    end(copies)
    n = outs[0].shape[0]
    for k, dst in enumerate(outs):
        dst[...] = whole[k * n:(k + 1) * n].astype(F32)
    yield


def body(fields, down_weight, mid_weight, up_weight, cotangent):
    _, rows, full, ch = fields.shape
    half, cols = rows // 2, full // 2
    wide = cols + 2 * EDGE
    n_lat, n_lon = lax.axis_size("lat"), lax.axis_size("lon")
    cells = lax.axis_size("dp") * rows * n_lat * full * n_lon
    scale = 1.0 / math.sqrt(cells)
    k = 2 * ch
    vm = pl.BlockSpec(memory_space=pltpu.VMEM)

    def sds(shape, dtype=BF):
        return jax.ShapeDtypeStruct(shape, dtype)

    f, c = fields[0], cotangent[0]
    unit = n_lat * n_lon * 16
    taps = 9 * (ch // 2)

    def sums(count):
        padded = -(-count * taps // unit) * unit
        share, piece = padded // n_lon, padded // (n_lon * n_lat)
        return [
            pltpu.VMEM((2, padded, ch), BF),
            pltpu.VMEM((padded, ch), BF),
            pltpu.VMEM((padded, ch), BF),
            pltpu.VMEM((n_lon - 1, share, ch), BF),
            pltpu.VMEM((share, ch), BF),
            pltpu.VMEM((n_lat - 1, piece, ch), BF),
            pltpu.VMEM((padded, ch), BF),
            pltpu.VMEM((padded, ch), F32),
        ]

    count = 16 + 2 * (1 + 2 * (n_lon - 1) + 2 * (n_lat - 1))
    hbm = pl.BlockSpec(memory_space=pl.ANY)
    out, gout, *terms = pl.pallas_call(
        functools.partial(level, scale),
        out_shape=(sds((rows, full, ch)), sds((rows, full, ch))) + (sds((taps, ch), F32),) * 3,
        in_specs=[hbm] * 5,
        out_specs=(vm,) * 5,
        scratch_shapes=[
            pltpu.VMEM((rows, full, ch), BF),
            pltpu.VMEM((rows, full, ch), BF),
            pltpu.VMEM((2, 2, 8, full, ch), BF),
            pltpu.VMEM((half, 16, ch), BF),
            pltpu.VMEM((half, 16, ch), BF),
            pltpu.VMEM((half // 2, 16, ch), BF),
            pltpu.VMEM((2, 4, 16, ch), BF),
            pltpu.VMEM((2, 4, 16, ch), BF),
            pltpu.VMEM((2, 2, 16, ch), BF),
            pltpu.VMEM((half, 16, ch), BF),
            pltpu.VMEM((half, 16, ch), BF),
            pltpu.VMEM((half // 2, 16, ch), BF),
            pltpu.VMEM((3, 3, 3, ch, ch), BF),
            pltpu.SemaphoreType.DMA((5,)),
            pltpu.SemaphoreType.DMA((count,)),
            pltpu.SemaphoreType.DMA((count,)),
            pltpu.VMEM((half + 9, 2, wide, k), BF),
            pltpu.VMEM((half + 9, 2, wide, k), BF),
            pltpu.VMEM((8, full + 4 * HALO, ch), F32),
            pltpu.VMEM((8, 2, full, ch), F32),
            pltpu.VMEM((3 * k, k), BF),
            pltpu.VMEM((3 * k, k), BF),
            pltpu.VMEM((2 * k, 3 * k), BF),
            pltpu.VMEM((2 * k, 3 * k), BF),
            pltpu.VMEM((3 * k, k), BF),
            pltpu.VMEM((3 * k, k), BF),
            pltpu.VMEM(((half + 8) // 2, wide, k), BF),
            pltpu.VMEM(((half + 4) // 2, 2, wide, 3 * ch), BF),
            pltpu.VMEM(((half + 4) // 2, wide, k), BF),
            pltpu.VMEM(((half + 4) // 2, 2, wide, k), BF),
            pltpu.VMEM(((half + 2) // 2, 2, wide, k), BF),
            pltpu.VMEM((k, 3 * k), F32),
            pltpu.VMEM((3 * ch, 3 * ch), F32),
            pltpu.VMEM((k, 3 * k), F32),
        ] + sums(2) + sums(1),
        compiler_params=pltpu.CompilerParams(
            collective_id=0, has_side_effects=True, vmem_limit_bytes=56 << 20),
    )(f, c, down_weight, mid_weight, up_weight)
    return (out[None], gout[None]) + tuple(t.reshape(3, 3, ch // 2, ch) for t in terms)


def solution(mesh):
    maps = P("dp", "lat", "lon", None)
    kernel = P(None, None, "dp", None)
    return jax.shard_map(
        body,
        mesh=mesh,
        in_specs=(maps, kernel, kernel, kernel, maps),
        out_specs=(maps, maps, kernel, kernel, kernel),
        check_vma=False,
    )
```

```python
import functools
import math

import jax
import jax.numpy as jnp
from jax import lax
from jax.experimental import pallas as pl
from jax.experimental.pallas import tpu as pltpu
from jax.sharding import PartitionSpec as P

EDGE = 8
HALO = 8
BF = jnp.bfloat16
F32 = jnp.float32


def dot(a, b):
    return lax.dot_general(a, b, (((1,), (0,)), ((), ())), preferred_element_type=F32)


def dot_t(a, b):
    return lax.dot_general(a, b, (((0,), (0,)), ((), ())), preferred_element_type=F32)


def rolled(x, by):
    return pltpu.roll(x, by % x.shape[0], 0)


def lanes(*parts):
    return jnp.concatenate(parts, axis=-1)


def blocks(rows):
    return jnp.concatenate([lanes(*row) for row in rows], axis=0)


def strided_block(w, r, z):
    return blocks([[w(r, 1), z], [w(r, 2), w(r, 0)]])


def spread_block(w, r, z):
    return blocks([[w(r, 1), w(r, 2)], [z, w(r, 0)]])


def paired_block(w, c, z):
    return blocks([[w(0, c), z], [w(1, c), w(0, c)], [w(2, c), w(1, c)], [z, w(2, c)]])


def flat(x):
    return x.reshape(x.shape[0] * x.shape[1], x.shape[2])


def level(scale, f_in, c_in, wd_in, wm_in, wu_in, out_hbm, gout_hbm, down_out, mid_out, up_out,
          out, gout, leave,
          raw_f, raw_c, rows_in, low_in, high_in, pair_in, low_at, high_at, pair_at,
          low_out, high_out, pair_out, w_in, local, send, recv,
          f, c, tmp, otmp, bd, bg, bm, bn, bu, bf, dp, gps, gpp, s1, s2, acc_u, acc_m, acc_d,
          *sums):
    rows = raw_f.shape[0]
    half = rows // 2
    wd, wm, wu = w_in.at[0], w_in.at[1], w_in.at[2]
    wide = f.shape[2]
    ch = f.shape[3] // 2
    cols = wide - 2 * EDGE
    z = jnp.zeros((ch, ch), BF)
    lat = lax.axis_index("lat")
    lon, core = lax.axis_index("lon"), lax.axis_index("dp")
    n_lat, n_lon = lax.axis_size("lat"), lax.axis_size("lon")
    other = 1 - core
    below, above = lat > 0, lat < n_lat - 1
    low = jnp.where(below, -(1 << 20), 0)
    high = jnp.where(above, 1 << 20, half)
    full = 2 * cols
    east = [lax.rem(lon + k, n_lon) for k in range(1, n_lon)]
    north = [lax.rem(lat + k, n_lat) for k in range(1, n_lat)]

    rows_in[...] = jnp.zeros_like(rows_in)
    for ref in (low_at, high_at, pair_at):
        ref[...] = jnp.zeros_like(ref)

    barrier = pltpu.get_barrier_semaphore()

    def greet(**where):
        pl.semaphore_signal(barrier, inc=1, device_id=where, device_id_type=pl.DeviceIdType.MESH)

    greet(dp=other)
    for p in east:
        greet(lon=p)
    for p in north:
        greet(lat=p)
    for ok, to in ((below, lat - 1), (above, lat + 1)):
        @pl.when(ok)
        def _(to=to):
            greet(lat=to, lon=east[0])
            greet(lat=to, lon=east[-1])

    part = ch // 2
    mine = pl.ds(pl.multiple_of(core * part, part), part)
    loads = []
    for place in (pl.ds(0, 16), pl.ds(full - 16, 16), pl.ds(16, full - 32)):
        for src, dst in ((f_in, raw_f), (c_in, raw_c)):
            loads.append(pltpu.make_async_copy(src.at[:, place], dst.at[:, place], local.at[len(loads)]))
    for i, w in enumerate((wd_in, wm_in, wu_in)):
        loads.append(pltpu.make_async_copy(w, w_in.at[i, :, :, mine, :], local.at[len(loads)]))
    for load in loads:
        load.start()
    pl.semaphore_wait(barrier, n_lon + n_lat - 1 + 2 * below.astype(jnp.int32) + 2 * above.astype(jnp.int32))

    used = [0]

    def remote(src, dst, **where):
        i = used[0]
        used[0] += 1
        return pltpu.make_async_remote_copy(
            src_ref=src, dst_ref=dst, send_sem=send.at[i], recv_sem=recv.at[i],
            device_id=where, device_id_type=pl.DeviceIdType.MESH)

    def under(condition, act):
        if condition is None:
            act()
        else:
            pl.when(condition)(act)

    halos = []
    for k, w in enumerate((wd_in, wm_in, wu_in)):
        halos.append((remote(w, w_in.at[k, :, :, mine, :], dp=other), None, None))
    for a, src in enumerate((f_in, c_in)):
        n0, n1 = (5, 6) if a == 0 else (3, 4)
        halos.append((remote(src.at[pl.ds(rows - n0, n0)], rows_in.at[a, 0, pl.ds(8 - n0, n0)], lat=lat + 1), above, below))
        halos.append((remote(src.at[pl.ds(0, n1)], rows_in.at[a, 1, pl.ds(0, n1)], lat=lat - 1), below, above))
    early = len(halos)
    for copy, sends, _ in halos:
        under(sends, copy.start)

    for load in loads[:4]:
        load.wait()

    def slots(n):
        return lax.broadcasted_iota(jnp.int32, (n, HALO, ch), 1)

    x_f = raw_f[:, full - 16:, :].astype(F32)[:, 8:]
    x_c = raw_c[:, full - 16:, :].astype(F32)[:, 8:]
    x = jnp.where(slots(rows) < 5, pltpu.roll(x_f, 5, 1), x_c)
    low_out[...] = x.reshape(half, 16, ch).astype(BF)
    high_out[...] = raw_f[:, :16, :].astype(F32)[:, :8].reshape(half, 16, ch).astype(BF)
    x = raw_c[:, :16, :].astype(F32)[:, :8].reshape(half, 2, HALO, ch)
    x = jnp.where(slots(half) < 4, x[:, 0], pltpu.roll(x[:, 1], 4, 1))
    pair_out[...] = x.reshape(half // 2, 16, ch).astype(BF)

    halos.append((remote(low_out, low_in, lon=east[0]), None, None))
    halos.append((remote(high_out, high_in, lon=east[-1]), None, None))
    halos.append((remote(pair_out, pair_in, lon=east[-1]), None, None))
    for d, to, sends, gets in ((0, lat + 1, above, below), (1, lat - 1, below, above)):
        begin = half - 4 if d == 0 else 0
        here = pl.ds(begin, 4)
        halos.append((remote(low_out.at[here], low_at.at[d], lat=to, lon=east[0]), sends, gets))
        halos.append((remote(high_out.at[here], high_at.at[d], lat=to, lon=east[-1]), sends, gets))
        here = pl.ds(begin // 2, 2)
        halos.append((remote(pair_out.at[here], pair_at.at[d], lat=to, lon=east[-1]), sends, gets))
    for copy, sends, _ in halos[early:]:
        under(sends, copy.start)
    for load in loads[4:]:
        load.wait()

    def landed(part_of):
        for copy, sends, gets in part_of:
            under(sends, copy.wait_send)
            under(gets, copy.wait_recv)

    def plain(ref):
        return lambda r, k: ref[r, k]

    def turned(ref):
        return lambda r, k: ref[r, k].T

    def flipped(ref):
        return lambda r, k: ref[2 - r, 2 - k].T

    def inside(at):
        return jnp.logical_and(at >= low, at < high)

    def pair_mask(n, base):
        shape = (n, wide, 2 * ch)
        rows = (base + 2 * lax.broadcasted_iota(jnp.int32, shape, 0)
                + (lax.broadcasted_iota(jnp.int32, shape, 2) >= ch).astype(jnp.int32))
        return inside(rows)

    def strided(src, start, n, weight):
        x0 = src[pl.ds(start, n), 1]
        x1 = src[pl.ds(start + 1, n), 0]
        x2 = src[pl.ds(start + 1, n), 1]
        acc = dot(flat(lanes(x0, x1, x2)), weight[...])
        return acc[:, :ch] + rolled(acc[:, ch:], 1)

    def to_pairs(x, n):
        x = x.reshape(n, 2, wide, ch)
        return lanes(x[:, 0], x[:, 1])

    def same(src, start, n, weight):
        acc = dot(flat(lanes(src[pl.ds(start, n)], src[pl.ds(start + 1, n)])), weight[...])
        k = 2 * ch
        total = rolled(acc[:, :k], 1) + acc[:, k:2 * k] + rolled(acc[:, 2 * k:], -1)
        return total

    side = jnp.zeros((8, 2 * HALO, ch), F32)
    tmp[:, 0:2 * HALO, :] = side
    tmp[:, full + 2 * HALO:, :] = side

    def lay(dst, pair, middle):
        tmp[:, 2 * HALO:2 * HALO + full, :] = middle.astype(F32)
        even = tmp[:, pl.ds(0, wide, stride=2), :]
        odd = tmp[:, pl.ds(1, wide, stride=2), :]
        dst[pl.ds(pair, 4)] = lanes(even, odd).astype(BF).reshape(4, 2, wide, 2 * ch)

    def lay_step(t, _):
        lay(f, 4 * t + 4, raw_f[pl.ds(8 * t, 8)])
        lay(c, 4 * t + 4, raw_c[pl.ds(8 * t, 8)])
        return 0

    lax.fori_loop(0, half // 4, lay_step, 0)
    for dst in (f, c):
        dst[half + 8] = jnp.zeros((2, wide, 2 * ch), BF)

    landed(halos[:3])
    for r in range(3):
        at = pl.ds(2 * ch * r, 2 * ch)
        bd[at, :] = strided_block(plain(wd), r, z)
        bg[at, :] = strided_block(turned(wu), r, z)
        bu[at, :] = spread_block(plain(wu), r, z)
        bf[at, :] = spread_block(turned(wd), r, z)
        bm[:, at] = paired_block(plain(wm), r, z)
        bn[:, at] = paired_block(flipped(wm), r, z)

    landed(halos[3:early])
    for a, dst in enumerate((f, c)):
        lay(dst, 0, rows_in[a, 0])
        lay(dst, half + 4, rows_in[a, 1])

    landed(halos[early:])

    def edge(dst, pair, lower, upper):
        tmp[:, HALO:2 * HALO, :] = lower
        tmp[:, 3 * HALO:4 * HALO, :] = jnp.zeros_like(lower)
        tmp[:, 2 * HALO:3 * HALO, :] = upper
        at = pl.ds(pair, 4)
        new = lanes(tmp[:, pl.ds(0, HALO, stride=2), :], tmp[:, pl.ds(1, HALO, stride=2), :])
        old = dst[at, :, 0:16, :].astype(F32).reshape(8, 16, 2 * ch)
        dst[at, :, 0:16, :] = jnp.concatenate([new, old[:, 8:]], axis=1).astype(BF).reshape(4, 2, 16, 2 * ch)
        new = lanes(tmp[:, pl.ds(2 * HALO, HALO, stride=2), :], tmp[:, pl.ds(2 * HALO + 1, HALO, stride=2), :])
        old = dst[at, :, wide - 16:, :].astype(F32).reshape(8, 16, 2 * ch)
        dst[at, :, wide - 16:, :] = jnp.concatenate([old[:, :8], new], axis=1).astype(BF).reshape(4, 2, 16, 2 * ch)

    def edges(pair, lower, upper, paired):
        slot = slots(8)
        z8 = jnp.zeros((8, HALO, ch), F32)
        lower = lower.astype(F32).reshape(8, HALO, ch)
        upper = upper.astype(F32).reshape(8, HALO, ch)
        paired = paired.astype(F32).reshape(4, 1, HALO, ch)
        paired = jnp.concatenate([paired, pltpu.roll(paired.reshape(4, HALO, ch), 4, 1)[:, None]], axis=1)
        paired = paired.reshape(8, HALO, ch)
        edge(f, pair, jnp.where(slot >= 3, pltpu.roll(lower, 3, 1), z8), upper)
        edge(c, pair, jnp.where(slot >= 5, lower, z8), jnp.where(slot < 4, paired, z8))

    tmp[:, 0:HALO, :] = jnp.zeros((8, HALO, ch), F32)

    def edge_step(t, _):
        at = pl.ds(4 * t, 4)
        edges(4 * t + 4, low_in[at], high_in[at], pair_in[pl.ds(2 * t, 2)])
        return 0

    lax.fori_loop(0, half // 4, edge_step, 0)
    edges(0, low_at[0], high_at[0], pair_at[0])
    edges(half + 4, low_at[1], high_at[1], pair_at[1])

    pairs = (half + 8) // 2
    nd = 6 if pairs % 6 == 0 else 1

    def down_step(t, _):
        q = t * nd
        v = strided(f, 2 * q, 2 * nd, bd)
        v = to_pairs(v, nd)
        dp[pl.ds(q, nd)] = jnp.where(pair_mask(nd, 2 * q - 3), v, 0.0).astype(BF)
        return 0

    lax.fori_loop(0, pairs // nd, down_step, 0)

    def shifted_rows(dst, start, n, v):
        nxt = rolled(v, -1)
        for a in range(2):
            half_lanes = slice(a * ch, (a + 1) * ch)
            piece = lanes(v[:, half_lanes], nxt[:, half_lanes]).astype(BF)
            dst[pl.ds(start, n), a] = piece.reshape(n, wide, 2 * ch)

    pairs_mid = (half + 4) // 2
    nm = 11 if pairs_mid % 11 == 0 else 1

    def mid_step(t, _):
        p = t * nm
        pre = same(dp, p, nm, bm)
        g = strided(c, 2 * p + 1, 2 * nm, bg)
        g = flat(to_pairs(g, nm))
        sig = jax.nn.sigmoid(pre)
        ok = flat(pair_mask(nm, 2 * p - 2))
        mid = jnp.where(ok, pre * sig, 0.0)
        gp = jnp.where(ok, g * sig * (1.0 + pre * (1.0 - sig)), 0.0)
        shifted_rows(s1, p, nm, mid)
        gpp[pl.ds(p, nm)] = gp.astype(BF).reshape(nm, wide, 2 * ch)
        place = lax.broadcasted_iota(jnp.int32, (nm, wide, 2 * ch), 1)
        own = flat(jnp.logical_and(place >= EDGE, place < EDGE + cols))
        gm = jnp.where(own, gp, 0.0)
        after, before = rolled(gm, -1), rolled(gm, 1)
        for a in range(2):
            k = slice(a * ch, (a + 1) * ch)
            piece = lanes(after[:, k], gm[:, k], before[:, k]).astype(BF)
            gps[pl.ds(p, nm), a] = piece.reshape(nm, wide, 3 * ch)
        return 0

    lax.fori_loop(0, pairs_mid // nm, mid_step, 0)

    acc_u[...] = jnp.zeros_like(acc_u)
    acc_m[...] = jnp.zeros_like(acc_m)
    acc_d[...] = jnp.zeros_like(acc_d)
    place = lax.broadcasted_iota(jnp.int32, (wide, 2 * ch), 0)
    place = place + (lax.broadcasted_iota(jnp.int32, (wide, 2 * ch), 1) >= ch).astype(jnp.int32)
    own = jnp.logical_and(place >= EDGE, place < EDGE + cols).astype(F32).astype(BF)[None]
    step = 4

    def taps(src, i, n):
        return flat(lanes(src[pl.ds(i + 3, n), 1], src[pl.ds(i + 4, n), 0], src[pl.ds(i + 4, n), 1]))

    def first_grads(t, _):
        p = t * step
        n = 2 * step
        m = s1[pl.ds(p + 1, step)].reshape(n, wide, 2 * ch) * own
        acc_u[...] += dot_t(flat(m), taps(c, 2 * p, n))
        d0, d1 = dp[pl.ds(p + 1, step)], dp[pl.ds(p + 2, step)]
        acc_m[...] += (
            dot_t(flat(gps[pl.ds(p + 1, step), 0]), flat(lanes(d0, d1[:, :, :ch])))
            + dot_t(flat(gps[pl.ds(p + 1, step), 1]), flat(lanes(d0[:, :, ch:], d1)))
        )
        return 0

    def last_grads(t, _):
        p = t * step
        n = 2 * step
        ga = s2[pl.ds(p, step + 1)].reshape(2 * step + 2, wide, 2 * ch)[1:1 + n] * own
        acc_d[...] += dot_t(flat(ga), taps(f, 2 * p, n))
        return 0

    def put(grads, tap, value):
        value = value.astype(BF)
        for h in range(2):
            grads[h, tap * part:(tap + 1) * part, :] = value[h * part:(h + 1) * part]

    def clear(grads, count):
        rest = grads.shape[1] - count * part
        if rest:
            grads[:, count * part:, :] = jnp.zeros((2, rest, ch), BF)

    batch_a = total_of(remote, sums[:8], (mid_out, up_out), lat, lon, core, north, east)
    batch_b = total_of(remote, sums[8:], (down_out,), lat, lon, core, north, east)

    lax.fori_loop(0, half // (2 * step), first_grads, 0)
    where = [(r, k, ch if k == 0 else 0, 2 * ch * r + (0 if k == 1 else ch)) for r in range(3) for k in range(3)]
    for r, k, top, left in where:
        tap = 3 * r + k
        put(sums[0], tap, (acc_m[k * ch:(k + 1) * ch, r * ch:(r + 1) * ch] * scale).T)
        put(sums[0], 9 + tap, acc_u[top:top + ch, left:left + ch] * scale)
    clear(sums[0], 18)
    next(batch_a)

    pairs_gd = (half + 2) // 2
    ng = 7 if pairs_gd % 7 == 0 else 1

    def gd_step(t, _):
        q = t * ng
        v = same(gpp, q, ng, bn)
        v = jnp.where(flat(pair_mask(ng, 2 * q - 1)), v, 0.0)
        shifted_rows(s2, q, ng, v)
        return 0

    lax.fori_loop(0, 1, gd_step, 0)
    next(batch_a)
    lax.fori_loop(1, pairs_gd // ng, gd_step, 0)
    lax.fori_loop(0, half // (2 * step), last_grads, 0)
    for r, k, top, left in where:
        put(sums[8], 3 * r + k, (acc_d[top:top + ch, left:left + ch] * scale).T)
    clear(sums[8], 9)
    next(batch_b)
    next(batch_a)

    def up_step(t, _):
        i = t * n_up
        def rows1(at, n):
            q = t * (n_up // 2) + 1
            return s1[pl.ds(q, n // 2 + 1)].reshape(n + 2, wide, 2 * ch)[at:at + n]
        def rows2(at, n):
            q = t * (n_up // 2)
            return s2[pl.ds(q, n // 2 + 1)].reshape(n + 2, wide, 2 * ch)[at + 1:at + 1 + n]
        for rows, base, dst, weight in ((rows1, raw_f, out, bu), (rows2, raw_c, gout, bf)):
            lo, hi = flat(rows(0, n_up)), flat(rows(1, n_up))
            k = 2 * ch
            even = dot(lo, weight[k:2 * k, :])
            odd = dot(lo, weight[2 * k:, :]) + dot(hi, weight[:k, :])
            for a, v in enumerate((even, odd)):
                v = v.reshape(n_up, wide, k)[:, EDGE:EDGE + cols]
                otmp[:, a, pl.ds(0, cols, stride=2), :] = v[:, :, :ch]
                otmp[:, a, pl.ds(1, cols, stride=2), :] = v[:, :, ch:]
            at = pl.ds(2 * i, 2 * n_up)
            total = base[at].astype(F32) + otmp[...].reshape(2 * n_up, full, ch)
            dst[at] = total.astype(BF)
        return 0

    n_up = 8
    steps = half // n_up
    cuts = [steps * i // 5 for i in range(6)]
    leaving = []
    for i in range(5):
        lax.fori_loop(cuts[i], cuts[i + 1], up_step, 0)
        band = pl.ds(cuts[i] * 2 * n_up, (cuts[i + 1] - cuts[i]) * 2 * n_up)
        for src, dst in ((out, out_hbm), (gout, gout_hbm)):
            copy = pltpu.make_async_copy(src.at[band], dst.at[band], leave.at[len(leaving)])
            copy.start()
            leaving.append(copy)
        next(batch_b, None)
        next(batch_a, None)
    for copy in leaving:
        copy.wait()


def total_of(remote, refs, outs, lat, lon, core, north, east):
    g, got, st1, r2, st2, r3, whole, acc = refs
    share, piece = st2.shape[0], r3.shape[1]

    def at(index, size):
        return pl.ds(pl.multiple_of(index * size, 16), size)

    def begin(copies):
        for copy in copies:
            copy.start()
        return copies

    def end(copies):
        for copy in copies:
            copy.wait()

    copies = begin([remote(g.at[1 - core], got, dp=1 - core)])
    yield
    end(copies)
    total = g[core].astype(F32) + got[...].astype(F32)
    acc[...] = total
    st1[...] = total.astype(BF)
    copies = begin([remote(st1.at[at(p, share)], r2.at[k], lon=p) for k, p in enumerate(east)])
    yield
    end(copies)
    total = acc[at(lon, share)]
    for k in range(len(east)):
        total = total + r2[k].astype(F32)
    acc[0:share] = total
    st2[...] = total.astype(BF)
    copies = begin([remote(st2.at[at(p, piece)], r3.at[k], lat=p) for k, p in enumerate(north)])
    yield
    end(copies)
    total = acc[at(lat, piece)]
    for k in range(len(north)):
        total = total + r3[k].astype(F32)
    own = pl.ds(pl.multiple_of(lon * share + lat * piece, 16), piece)
    whole[own] = total.astype(BF)
    copies = begin([remote(whole.at[own], whole.at[own], lat=p) for p in north])
    yield
    end(copies)
    band = at(lon, share)
    copies = begin([remote(whole.at[band], whole.at[band], lon=p) for p in east])
    yield
    end(copies)
    n = outs[0].shape[0]
    for k, dst in enumerate(outs):
        dst[...] = whole[k * n:(k + 1) * n].astype(F32)
    yield


def handed_on(*refs):
    count = len(refs) // 2
    for src, dst in zip(refs[:count], refs[count:]):
        dst[...] = src[...]


def body(fields, down_weight, mid_weight, up_weight, cotangent):
    _, rows, full, ch = fields.shape
    half, cols = rows // 2, full // 2
    wide = cols + 2 * EDGE
    n_lat, n_lon = lax.axis_size("lat"), lax.axis_size("lon")
    cells = lax.axis_size("dp") * rows * n_lat * full * n_lon
    scale = 1.0 / math.sqrt(cells)
    k = 2 * ch
    vm = pl.BlockSpec(memory_space=pltpu.VMEM)

    def sds(shape, dtype=BF):
        return jax.ShapeDtypeStruct(shape, dtype)

    f, c = fields[0], cotangent[0]
    unit = n_lat * n_lon * 16
    taps = 9 * (ch // 2)

    def sums(count):
        padded = -(-count * taps // unit) * unit
        share, piece = padded // n_lon, padded // (n_lon * n_lat)
        return [
            pltpu.VMEM((2, padded, ch), BF),
            pltpu.VMEM((padded, ch), BF),
            pltpu.VMEM((padded, ch), BF),
            pltpu.VMEM((n_lon - 1, share, ch), BF),
            pltpu.VMEM((share, ch), BF),
            pltpu.VMEM((n_lat - 1, piece, ch), BF),
            pltpu.VMEM((padded, ch), BF),
            pltpu.VMEM((padded, ch), F32),
        ]

    count = 16 + 2 * (1 + 2 * (n_lon - 1) + 2 * (n_lat - 1))
    hbm = pl.BlockSpec(memory_space=pl.ANY)
    out, gout, *terms = pl.pallas_call(
        functools.partial(level, scale),
        out_shape=(sds((rows, full, ch)), sds((rows, full, ch))) + (sds((taps, ch), F32),) * 3,
        in_specs=[hbm] * 5,
        out_specs=(hbm,) * 2 + (vm,) * 3,
        scratch_shapes=[
            pltpu.VMEM((rows, full, ch), BF),
            pltpu.VMEM((rows, full, ch), BF),
            pltpu.SemaphoreType.DMA((10,)),
            pltpu.VMEM((rows, full, ch), BF),
            pltpu.VMEM((rows, full, ch), BF),
            pltpu.VMEM((2, 2, 8, full, ch), BF),
            pltpu.VMEM((half, 16, ch), BF),
            pltpu.VMEM((half, 16, ch), BF),
            pltpu.VMEM((half // 2, 16, ch), BF),
            pltpu.VMEM((2, 4, 16, ch), BF),
            pltpu.VMEM((2, 4, 16, ch), BF),
            pltpu.VMEM((2, 2, 16, ch), BF),
            pltpu.VMEM((half, 16, ch), BF),
            pltpu.VMEM((half, 16, ch), BF),
            pltpu.VMEM((half // 2, 16, ch), BF),
            pltpu.VMEM((3, 3, 3, ch, ch), BF),
            pltpu.SemaphoreType.DMA((9,)),
            pltpu.SemaphoreType.DMA((count,)),
            pltpu.SemaphoreType.DMA((count,)),
            pltpu.VMEM((half + 9, 2, wide, k), BF),
            pltpu.VMEM((half + 9, 2, wide, k), BF),
            pltpu.VMEM((8, full + 4 * HALO, ch), F32),
            pltpu.VMEM((8, 2, full, ch), F32),
            pltpu.VMEM((3 * k, k), BF),
            pltpu.VMEM((3 * k, k), BF),
            pltpu.VMEM((2 * k, 3 * k), BF),
            pltpu.VMEM((2 * k, 3 * k), BF),
            pltpu.VMEM((3 * k, k), BF),
            pltpu.VMEM((3 * k, k), BF),
            pltpu.VMEM(((half + 8) // 2, wide, k), BF),
            pltpu.VMEM(((half + 4) // 2, 2, wide, 3 * ch), BF),
            pltpu.VMEM(((half + 4) // 2, wide, k), BF),
            pltpu.VMEM(((half + 4) // 2, 2, wide, k), BF),
            pltpu.VMEM(((half + 2) // 2, 2, wide, k), BF),
            pltpu.VMEM((k, 3 * k), F32),
            pltpu.VMEM((3 * ch, 3 * ch), F32),
            pltpu.VMEM((k, 3 * k), F32),
        ] + sums(2) + sums(1),
        compiler_params=pltpu.CompilerParams(
            collective_id=0, has_side_effects=True, vmem_limit_bytes=56 << 20),
    )(f, c, down_weight, mid_weight, up_weight)
    results = (out, gout, *terms)

    def blocked(x):
        shape = (x.shape[0] // 4,) + x.shape[1:]
        return pl.BlockSpec(shape, lambda i: (i,) + (0,) * (len(shape) - 1))

    specs = tuple(blocked(x) for x in results)
    out, gout, *terms = pl.pallas_call(
        handed_on,
        grid=(4,),
        out_shape=tuple(sds(x.shape, x.dtype) for x in results),
        in_specs=list(specs),
        out_specs=specs,
        compiler_params=pltpu.CompilerParams(vmem_limit_bytes=56 << 20),
    )(*results)
    return (out[None], gout[None]) + tuple(t.reshape(3, 3, ch // 2, ch) for t in terms)


def solution(mesh):
    maps = P("dp", "lat", "lon", None)
    kernel = P(None, None, "dp", None)
    return jax.shard_map(
        body,
        mesh=mesh,
        in_specs=(maps, kernel, kernel, kernel, maps),
        out_specs=(maps, maps, kernel, kernel, kernel),
        check_vma=False,
    )
```

```python
import functools
import math

import jax
import jax.numpy as jnp
from jax import lax
from jax.experimental import pallas as pl
from jax.experimental.pallas import tpu as pltpu
from jax.sharding import PartitionSpec as P

EDGE = 8
HALO = 8
BF = jnp.bfloat16
F32 = jnp.float32


def dot(a, b):
    return lax.dot_general(a, b, (((1,), (0,)), ((), ())), preferred_element_type=F32)


def dot_t(a, b):
    return lax.dot_general(a, b, (((0,), (0,)), ((), ())), preferred_element_type=F32)


def rolled(x, by):
    return pltpu.roll(x, by % x.shape[0], 0)


def lanes(*parts):
    return jnp.concatenate(parts, axis=-1)


def blocks(rows):
    return jnp.concatenate([lanes(*row) for row in rows], axis=0)


def strided_block(w, r, z):
    return blocks([[w(r, 1), z], [w(r, 2), w(r, 0)]])


def spread_block(w, r, z):
    return blocks([[w(r, 1), w(r, 2)], [z, w(r, 0)]])


def paired_block(w, c, z):
    return blocks([[w(0, c), z], [w(1, c), w(0, c)], [w(2, c), w(1, c)], [z, w(2, c)]])


def flat(x):
    return x.reshape(x.shape[0] * x.shape[1], x.shape[2])


def level(scale, f_in, c_in, wd_in, wm_in, wu_in, out_hbm, gout_hbm, down_out, mid_out, up_out,
          out, gout, leave,
          raw_f, raw_c, rows_in, low_in, high_in, pair_in, low_at, high_at, pair_at,
          low_out, high_out, pair_out, w_in, local, send, recv,
          f, c, tmp, otmp, bd, bg, bm, bn, bu, bf, dp, gps, gpp, s1, s2, acc_u, acc_m, acc_d,
          *sums):
    rows = raw_f.shape[0]
    half = rows // 2
    wd, wm, wu = w_in.at[0], w_in.at[1], w_in.at[2]
    wide = f.shape[2]
    ch = f.shape[3] // 2
    cols = wide - 2 * EDGE
    z = jnp.zeros((ch, ch), BF)
    lat = lax.axis_index("lat")
    lon, core = lax.axis_index("lon"), lax.axis_index("dp")
    n_lat, n_lon = lax.axis_size("lat"), lax.axis_size("lon")
    other = 1 - core
    below, above = lat > 0, lat < n_lat - 1
    low = jnp.where(below, -(1 << 20), 0)
    high = jnp.where(above, 1 << 20, half)
    full = 2 * cols
    east = [lax.rem(lon + k, n_lon) for k in range(1, n_lon)]
    north = [lax.rem(lat + k, n_lat) for k in range(1, n_lat)]

    rows_in[...] = jnp.zeros_like(rows_in)
    for ref in (low_at, high_at, pair_at):
        ref[...] = jnp.zeros_like(ref)

    barrier = pltpu.get_barrier_semaphore()

    def greet(**where):
        pl.semaphore_signal(barrier, inc=1, device_id=where, device_id_type=pl.DeviceIdType.MESH)

    greet(dp=other)
    for p in east:
        greet(lon=p)
    for p in north:
        greet(lat=p)
    for ok, to in ((below, lat - 1), (above, lat + 1)):
        @pl.when(ok)
        def _(to=to):
            greet(lat=to, lon=east[0])
            greet(lat=to, lon=east[-1])

    part = ch // 2
    mine = pl.ds(pl.multiple_of(core * part, part), part)
    loads = []
    for place in (pl.ds(0, 16), pl.ds(full - 16, 16), pl.ds(16, full - 32)):
        for src, dst in ((f_in, raw_f), (c_in, raw_c)):
            loads.append(pltpu.make_async_copy(src.at[:, place], dst.at[:, place], local.at[len(loads)]))
    for i, w in enumerate((wd_in, wm_in, wu_in)):
        loads.append(pltpu.make_async_copy(w, w_in.at[i, :, :, mine, :], local.at[len(loads)]))
    for load in loads:
        load.start()
    pl.semaphore_wait(barrier, n_lon + n_lat - 1 + 2 * below.astype(jnp.int32) + 2 * above.astype(jnp.int32))

    used = [0]

    def remote(src, dst, **where):
        i = used[0]
        used[0] += 1
        return pltpu.make_async_remote_copy(
            src_ref=src, dst_ref=dst, send_sem=send.at[i], recv_sem=recv.at[i],
            device_id=where, device_id_type=pl.DeviceIdType.MESH)

    def under(condition, act):
        if condition is None:
            act()
        else:
            pl.when(condition)(act)

    halos = []
    for k, w in enumerate((wd_in, wm_in, wu_in)):
        halos.append((remote(w, w_in.at[k, :, :, mine, :], dp=other), None, None))
    for a, src in enumerate((f_in, c_in)):
        n0, n1 = (5, 6) if a == 0 else (3, 4)
        halos.append((remote(src.at[pl.ds(rows - n0, n0)], rows_in.at[a, 0, pl.ds(8 - n0, n0)], lat=lat + 1), above, below))
        halos.append((remote(src.at[pl.ds(0, n1)], rows_in.at[a, 1, pl.ds(0, n1)], lat=lat - 1), below, above))
    early = len(halos)
    for copy, sends, _ in halos:
        under(sends, copy.start)

    for load in loads[:4]:
        load.wait()

    def slots(n):
        return lax.broadcasted_iota(jnp.int32, (n, HALO, ch), 1)

    x_f = raw_f[:, full - 16:, :].astype(F32)[:, 8:]
    x_c = raw_c[:, full - 16:, :].astype(F32)[:, 8:]
    x = jnp.where(slots(rows) < 5, pltpu.roll(x_f, 5, 1), x_c)
    low_out[...] = x.reshape(half, 16, ch).astype(BF)
    high_out[...] = raw_f[:, :16, :].astype(F32)[:, :8].reshape(half, 16, ch).astype(BF)
    x = raw_c[:, :16, :].astype(F32)[:, :8].reshape(half, 2, HALO, ch)
    x = jnp.where(slots(half) < 4, x[:, 0], pltpu.roll(x[:, 1], 4, 1))
    pair_out[...] = x.reshape(half // 2, 16, ch).astype(BF)

    halos.append((remote(low_out, low_in, lon=east[0]), None, None))
    halos.append((remote(high_out, high_in, lon=east[-1]), None, None))
    halos.append((remote(pair_out, pair_in, lon=east[-1]), None, None))
    for d, to, sends, gets in ((0, lat + 1, above, below), (1, lat - 1, below, above)):
        begin = half - 4 if d == 0 else 0
        here = pl.ds(begin, 4)
        halos.append((remote(low_out.at[here], low_at.at[d], lat=to, lon=east[0]), sends, gets))
        halos.append((remote(high_out.at[here], high_at.at[d], lat=to, lon=east[-1]), sends, gets))
        here = pl.ds(begin // 2, 2)
        halos.append((remote(pair_out.at[here], pair_at.at[d], lat=to, lon=east[-1]), sends, gets))
    for copy, sends, _ in halos[early:]:
        under(sends, copy.start)
    for load in loads[4:]:
        load.wait()

    def landed(part_of):
        for copy, sends, gets in part_of:
            under(sends, copy.wait_send)
            under(gets, copy.wait_recv)

    def plain(ref):
        return lambda r, k: ref[r, k]

    def turned(ref):
        return lambda r, k: ref[r, k].T

    def flipped(ref):
        return lambda r, k: ref[2 - r, 2 - k].T

    def inside(at):
        return jnp.logical_and(at >= low, at < high)

    def pair_mask(n, base):
        shape = (n, wide, 2 * ch)
        rows = (base + 2 * lax.broadcasted_iota(jnp.int32, shape, 0)
                + (lax.broadcasted_iota(jnp.int32, shape, 2) >= ch).astype(jnp.int32))
        return inside(rows)

    def strided(src, start, n, weight):
        x0 = src[pl.ds(start, n), 1]
        x1 = src[pl.ds(start + 1, n), 0]
        x2 = src[pl.ds(start + 1, n), 1]
        acc = dot(flat(lanes(x0, x1, x2)), weight[...])
        return acc[:, :ch] + rolled(acc[:, ch:], 1)

    def to_pairs(x, n):
        x = x.reshape(n, 2, wide, ch)
        return lanes(x[:, 0], x[:, 1])

    def same(src, start, n, weight):
        acc = dot(flat(lanes(src[pl.ds(start, n)], src[pl.ds(start + 1, n)])), weight[...])
        k = 2 * ch
        total = rolled(acc[:, :k], 1) + acc[:, k:2 * k] + rolled(acc[:, 2 * k:], -1)
        return total

    side = jnp.zeros((8, 2 * HALO, ch), F32)
    tmp[:, 0:2 * HALO, :] = side
    tmp[:, full + 2 * HALO:, :] = side

    def lay(dst, pair, middle):
        tmp[:, 2 * HALO:2 * HALO + full, :] = middle.astype(F32)
        even = tmp[:, pl.ds(0, wide, stride=2), :]
        odd = tmp[:, pl.ds(1, wide, stride=2), :]
        dst[pl.ds(pair, 4)] = lanes(even, odd).astype(BF).reshape(4, 2, wide, 2 * ch)

    def lay_step(t, _):
        lay(f, 4 * t + 4, raw_f[pl.ds(8 * t, 8)])
        lay(c, 4 * t + 4, raw_c[pl.ds(8 * t, 8)])
        return 0

    lax.fori_loop(0, half // 4, lay_step, 0)
    for dst in (f, c):
        dst[half + 8] = jnp.zeros((2, wide, 2 * ch), BF)

    landed(halos[:3])
    for r in range(3):
        at = pl.ds(2 * ch * r, 2 * ch)
        bd[at, :] = strided_block(plain(wd), r, z)
        bg[at, :] = strided_block(turned(wu), r, z)
        bu[at, :] = spread_block(plain(wu), r, z)
        bf[at, :] = spread_block(turned(wd), r, z)
        bm[:, at] = paired_block(plain(wm), r, z)
        bn[:, at] = paired_block(flipped(wm), r, z)

    landed(halos[3:early])
    for a, dst in enumerate((f, c)):
        lay(dst, 0, rows_in[a, 0])
        lay(dst, half + 4, rows_in[a, 1])

    landed(halos[early:])

    def edge(dst, pair, lower, upper):
        tmp[:, HALO:2 * HALO, :] = lower
        tmp[:, 3 * HALO:4 * HALO, :] = jnp.zeros_like(lower)
        tmp[:, 2 * HALO:3 * HALO, :] = upper
        at = pl.ds(pair, 4)
        new = lanes(tmp[:, pl.ds(0, HALO, stride=2), :], tmp[:, pl.ds(1, HALO, stride=2), :])
        old = dst[at, :, 0:16, :].astype(F32).reshape(8, 16, 2 * ch)
        dst[at, :, 0:16, :] = jnp.concatenate([new, old[:, 8:]], axis=1).astype(BF).reshape(4, 2, 16, 2 * ch)
        new = lanes(tmp[:, pl.ds(2 * HALO, HALO, stride=2), :], tmp[:, pl.ds(2 * HALO + 1, HALO, stride=2), :])
        old = dst[at, :, wide - 16:, :].astype(F32).reshape(8, 16, 2 * ch)
        dst[at, :, wide - 16:, :] = jnp.concatenate([old[:, :8], new], axis=1).astype(BF).reshape(4, 2, 16, 2 * ch)

    def edges(pair, lower, upper, paired):
        slot = slots(8)
        z8 = jnp.zeros((8, HALO, ch), F32)
        lower = lower.astype(F32).reshape(8, HALO, ch)
        upper = upper.astype(F32).reshape(8, HALO, ch)
        paired = paired.astype(F32).reshape(4, 1, HALO, ch)
        paired = jnp.concatenate([paired, pltpu.roll(paired.reshape(4, HALO, ch), 4, 1)[:, None]], axis=1)
        paired = paired.reshape(8, HALO, ch)
        edge(f, pair, jnp.where(slot >= 3, pltpu.roll(lower, 3, 1), z8), upper)
        edge(c, pair, jnp.where(slot >= 5, lower, z8), jnp.where(slot < 4, paired, z8))

    tmp[:, 0:HALO, :] = jnp.zeros((8, HALO, ch), F32)

    def edge_step(t, _):
        at = pl.ds(4 * t, 4)
        edges(4 * t + 4, low_in[at], high_in[at], pair_in[pl.ds(2 * t, 2)])
        return 0

    lax.fori_loop(0, half // 4, edge_step, 0)
    edges(0, low_at[0], high_at[0], pair_at[0])
    edges(half + 4, low_at[1], high_at[1], pair_at[1])

    pairs = (half + 8) // 2
    nd = 6 if pairs % 6 == 0 else 1

    def down_step(t, _):
        q = t * nd
        v = strided(f, 2 * q, 2 * nd, bd)
        v = to_pairs(v, nd)
        dp[pl.ds(q, nd)] = jnp.where(pair_mask(nd, 2 * q - 3), v, 0.0).astype(BF)
        return 0

    lax.fori_loop(0, pairs // nd, down_step, 0)

    def shifted_rows(dst, start, n, v):
        nxt = rolled(v, -1)
        for a in range(2):
            half_lanes = slice(a * ch, (a + 1) * ch)
            piece = lanes(v[:, half_lanes], nxt[:, half_lanes]).astype(BF)
            dst[pl.ds(start, n), a] = piece.reshape(n, wide, 2 * ch)

    pairs_mid = (half + 4) // 2
    nm = 11 if pairs_mid % 11 == 0 else 1

    def mid_step(t, _):
        p = t * nm
        pre = same(dp, p, nm, bm)
        g = strided(c, 2 * p + 1, 2 * nm, bg)
        g = flat(to_pairs(g, nm))
        sig = jax.nn.sigmoid(pre)
        ok = flat(pair_mask(nm, 2 * p - 2))
        mid = jnp.where(ok, pre * sig, 0.0)
        gp = jnp.where(ok, g * sig * (1.0 + pre * (1.0 - sig)), 0.0)
        shifted_rows(s1, p, nm, mid)
        gpp[pl.ds(p, nm)] = gp.astype(BF).reshape(nm, wide, 2 * ch)
        place = lax.broadcasted_iota(jnp.int32, (nm, wide, 2 * ch), 1)
        own = flat(jnp.logical_and(place >= EDGE, place < EDGE + cols))
        gm = jnp.where(own, gp, 0.0)
        after, before = rolled(gm, -1), rolled(gm, 1)
        for a in range(2):
            k = slice(a * ch, (a + 1) * ch)
            piece = lanes(after[:, k], gm[:, k], before[:, k]).astype(BF)
            gps[pl.ds(p, nm), a] = piece.reshape(nm, wide, 3 * ch)
        return 0

    lax.fori_loop(0, pairs_mid // nm, mid_step, 0)

    acc_u[...] = jnp.zeros_like(acc_u)
    acc_m[...] = jnp.zeros_like(acc_m)
    acc_d[...] = jnp.zeros_like(acc_d)
    place = lax.broadcasted_iota(jnp.int32, (wide, 2 * ch), 0)
    place = place + (lax.broadcasted_iota(jnp.int32, (wide, 2 * ch), 1) >= ch).astype(jnp.int32)
    own = jnp.logical_and(place >= EDGE, place < EDGE + cols).astype(F32).astype(BF)[None]
    step = 4

    def taps(src, i, n):
        return flat(lanes(src[pl.ds(i + 3, n), 1], src[pl.ds(i + 4, n), 0], src[pl.ds(i + 4, n), 1]))

    def first_grads(t, _):
        p = t * step
        n = 2 * step
        m = s1[pl.ds(p + 1, step)].reshape(n, wide, 2 * ch) * own
        acc_u[...] += dot_t(flat(m), taps(c, 2 * p, n))
        d0, d1 = dp[pl.ds(p + 1, step)], dp[pl.ds(p + 2, step)]
        acc_m[...] += (
            dot_t(flat(gps[pl.ds(p + 1, step), 0]), flat(lanes(d0, d1[:, :, :ch])))
            + dot_t(flat(gps[pl.ds(p + 1, step), 1]), flat(lanes(d0[:, :, ch:], d1)))
        )
        return 0

    def last_grads(t, _):
        p = t * step
        n = 2 * step
        ga = s2[pl.ds(p, step + 1)].reshape(2 * step + 2, wide, 2 * ch)[1:1 + n] * own
        acc_d[...] += dot_t(flat(ga), taps(f, 2 * p, n))
        return 0

    def put(grads, tap, value):
        value = value.astype(BF)
        for h in range(2):
            grads[h, tap * part:(tap + 1) * part, :] = value[h * part:(h + 1) * part]

    def clear(grads, count):
        rest = grads.shape[1] - count * part
        if rest:
            grads[:, count * part:, :] = jnp.zeros((2, rest, ch), BF)

    batch_a = total_of(remote, sums[:8], (mid_out, up_out), lat, lon, core, north, east)
    batch_b = total_of(remote, sums[8:], (down_out,), lat, lon, core, north, east)

    lax.fori_loop(0, half // (2 * step), first_grads, 0)
    where = [(r, k, ch if k == 0 else 0, 2 * ch * r + (0 if k == 1 else ch)) for r in range(3) for k in range(3)]
    for r, k, top, left in where:
        tap = 3 * r + k
        put(sums[0], tap, (acc_m[k * ch:(k + 1) * ch, r * ch:(r + 1) * ch] * scale).T)
        put(sums[0], 9 + tap, acc_u[top:top + ch, left:left + ch] * scale)
    clear(sums[0], 18)
    next(batch_a)

    pairs_gd = (half + 2) // 2
    ng = 7 if pairs_gd % 7 == 0 else 1

    def gd_step(t, _):
        q = t * ng
        v = same(gpp, q, ng, bn)
        v = jnp.where(flat(pair_mask(ng, 2 * q - 1)), v, 0.0)
        shifted_rows(s2, q, ng, v)
        return 0

    lax.fori_loop(0, 1, gd_step, 0)
    next(batch_a)
    lax.fori_loop(1, pairs_gd // ng, gd_step, 0)
    lax.fori_loop(0, half // (2 * step), last_grads, 0)
    for r, k, top, left in where:
        put(sums[8], 3 * r + k, (acc_d[top:top + ch, left:left + ch] * scale).T)
    clear(sums[8], 9)
    next(batch_b)
    next(batch_a)

    def up_step(t, _):
        i = t * n_up
        def rows1(at, n):
            q = t * (n_up // 2) + 1
            return s1[pl.ds(q, n // 2 + 1)].reshape(n + 2, wide, 2 * ch)[at:at + n]
        def rows2(at, n):
            q = t * (n_up // 2)
            return s2[pl.ds(q, n // 2 + 1)].reshape(n + 2, wide, 2 * ch)[at + 1:at + 1 + n]
        for rows, base, dst, weight in ((rows1, raw_f, out, bu), (rows2, raw_c, gout, bf)):
            lo, hi = flat(rows(0, n_up)), flat(rows(1, n_up))
            k = 2 * ch
            even = dot(lo, weight[k:2 * k, :])
            odd = dot(lo, weight[2 * k:, :]) + dot(hi, weight[:k, :])
            for a, v in enumerate((even, odd)):
                v = v.reshape(n_up, wide, k)[:, EDGE:EDGE + cols]
                otmp[:, a, pl.ds(0, cols, stride=2), :] = v[:, :, :ch]
                otmp[:, a, pl.ds(1, cols, stride=2), :] = v[:, :, ch:]
            at = pl.ds(2 * i, 2 * n_up)
            total = base[at].astype(F32) + otmp[...].reshape(2 * n_up, full, ch)
            dst[at] = total.astype(BF)
        return 0

    n_up = 8
    steps = half // n_up
    cuts = [steps * i // 5 for i in range(6)]
    leaving = []
    for i in range(5):
        lax.fori_loop(cuts[i], cuts[i + 1], up_step, 0)
        band = pl.ds(cuts[i] * 2 * n_up, (cuts[i + 1] - cuts[i]) * 2 * n_up)
        for src, dst in ((out, out_hbm), (gout, gout_hbm)):
            copy = pltpu.make_async_copy(src.at[band], dst.at[band], leave.at[len(leaving)])
            copy.start()
            leaving.append(copy)
        next(batch_b, None)
        next(batch_a, None)
    for copy in leaving:
        copy.wait()


def total_of(remote, refs, outs, lat, lon, core, north, east):
    g, got, st1, r2, st2, r3, whole, acc = refs
    share, piece = st2.shape[0], r3.shape[1]

    def at(index, size):
        return pl.ds(pl.multiple_of(index * size, 16), size)

    def begin(copies):
        for copy in copies:
            copy.start()
        return copies

    def end(copies):
        for copy in copies:
            copy.wait()

    copies = begin([remote(g.at[1 - core], got, dp=1 - core)])
    yield
    end(copies)
    total = g[core].astype(F32) + got[...].astype(F32)
    acc[...] = total
    st1[...] = total.astype(BF)
    copies = begin([remote(st1.at[at(p, share)], r2.at[k], lon=p) for k, p in enumerate(east)])
    yield
    end(copies)
    total = acc[at(lon, share)]
    for k in range(len(east)):
        total = total + r2[k].astype(F32)
    acc[0:share] = total
    st2[...] = total.astype(BF)
    copies = begin([remote(st2.at[at(p, piece)], r3.at[k], lat=p) for k, p in enumerate(north)])
    yield
    end(copies)
    total = acc[at(lat, piece)]
    for k in range(len(north)):
        total = total + r3[k].astype(F32)
    own = pl.ds(pl.multiple_of(lon * share + lat * piece, 16), piece)
    whole[own] = total.astype(BF)
    copies = begin([remote(whole.at[own], whole.at[own], lat=p) for p in north])
    yield
    end(copies)
    band = at(lon, share)
    copies = begin([remote(whole.at[band], whole.at[band], lon=p) for p in east])
    yield
    end(copies)
    n = outs[0].shape[0]
    for k, dst in enumerate(outs):
        dst[...] = whole[k * n:(k + 1) * n].astype(F32)
    yield


def handed_on(*refs):
    count = len(refs) // 2
    for src, dst in zip(refs[:count], refs[count:]):
        dst[...] = src[...]


def body(fields, down_weight, mid_weight, up_weight, cotangent):
    _, rows, full, ch = fields.shape
    half, cols = rows // 2, full // 2
    wide = cols + 2 * EDGE
    n_lat, n_lon = lax.axis_size("lat"), lax.axis_size("lon")
    cells = lax.axis_size("dp") * rows * n_lat * full * n_lon
    scale = 1.0 / math.sqrt(cells)
    k = 2 * ch
    vm = pl.BlockSpec(memory_space=pltpu.VMEM)

    def sds(shape, dtype=BF):
        return jax.ShapeDtypeStruct(shape, dtype)

    f, c = fields[0], cotangent[0]
    unit = n_lat * n_lon * 16
    taps = 9 * (ch // 2)

    def sums(count):
        padded = -(-count * taps // unit) * unit
        share, piece = padded // n_lon, padded // (n_lon * n_lat)
        return [
            pltpu.VMEM((2, padded, ch), BF),
            pltpu.VMEM((padded, ch), BF),
            pltpu.VMEM((padded, ch), BF),
            pltpu.VMEM((n_lon - 1, share, ch), BF),
            pltpu.VMEM((share, ch), BF),
            pltpu.VMEM((n_lat - 1, piece, ch), BF),
            pltpu.VMEM((padded, ch), BF),
            pltpu.VMEM((padded, ch), F32),
        ]

    count = 16 + 2 * (1 + 2 * (n_lon - 1) + 2 * (n_lat - 1))
    hbm = pl.BlockSpec(memory_space=pl.ANY)
    out, gout, *terms = pl.pallas_call(
        functools.partial(level, scale),
        out_shape=(sds((rows, full, ch)), sds((rows, full, ch))) + (sds((taps, ch), F32),) * 3,
        in_specs=[hbm] * 5,
        out_specs=(hbm,) * 2 + (vm,) * 3,
        scratch_shapes=[
            pltpu.VMEM((rows, full, ch), BF),
            pltpu.VMEM((rows, full, ch), BF),
            pltpu.SemaphoreType.DMA((10,)),
            pltpu.VMEM((rows, full, ch), BF),
            pltpu.VMEM((rows, full, ch), BF),
            pltpu.VMEM((2, 2, 8, full, ch), BF),
            pltpu.VMEM((half, 16, ch), BF),
            pltpu.VMEM((half, 16, ch), BF),
            pltpu.VMEM((half // 2, 16, ch), BF),
            pltpu.VMEM((2, 4, 16, ch), BF),
            pltpu.VMEM((2, 4, 16, ch), BF),
            pltpu.VMEM((2, 2, 16, ch), BF),
            pltpu.VMEM((half, 16, ch), BF),
            pltpu.VMEM((half, 16, ch), BF),
            pltpu.VMEM((half // 2, 16, ch), BF),
            pltpu.VMEM((3, 3, 3, ch, ch), BF),
            pltpu.SemaphoreType.DMA((9,)),
            pltpu.SemaphoreType.DMA((count,)),
            pltpu.SemaphoreType.DMA((count,)),
            pltpu.VMEM((half + 9, 2, wide, k), BF),
            pltpu.VMEM((half + 9, 2, wide, k), BF),
            pltpu.VMEM((8, full + 4 * HALO, ch), F32),
            pltpu.VMEM((8, 2, full, ch), F32),
            pltpu.VMEM((3 * k, k), BF),
            pltpu.VMEM((3 * k, k), BF),
            pltpu.VMEM((2 * k, 3 * k), BF),
            pltpu.VMEM((2 * k, 3 * k), BF),
            pltpu.VMEM((3 * k, k), BF),
            pltpu.VMEM((3 * k, k), BF),
            pltpu.VMEM(((half + 8) // 2, wide, k), BF),
            pltpu.VMEM(((half + 4) // 2, 2, wide, 3 * ch), BF),
            pltpu.VMEM(((half + 4) // 2, wide, k), BF),
            pltpu.VMEM(((half + 4) // 2, 2, wide, k), BF),
            pltpu.VMEM(((half + 2) // 2, 2, wide, k), BF),
            pltpu.VMEM((k, 3 * k), F32),
            pltpu.VMEM((3 * ch, 3 * ch), F32),
            pltpu.VMEM((k, 3 * k), F32),
        ] + sums(2) + sums(1),
        compiler_params=pltpu.CompilerParams(
            collective_id=0, has_side_effects=True, vmem_limit_bytes=56 << 20),
    )(f, c, down_weight, mid_weight, up_weight)
    results = (out, gout, *terms)

    def blocked(x):
        shape = (x.shape[0] // 8,) + x.shape[1:]
        return pl.BlockSpec(shape, lambda i: (i,) + (0,) * (len(shape) - 1))

    specs = tuple(blocked(x) for x in results)
    out, gout, *terms = pl.pallas_call(
        handed_on,
        grid=(8,),
        out_shape=tuple(sds(x.shape, x.dtype) for x in results),
        in_specs=list(specs),
        out_specs=specs,
        compiler_params=pltpu.CompilerParams(vmem_limit_bytes=56 << 20),
    )(*results)
    return (out[None], gout[None]) + tuple(t.reshape(3, 3, ch // 2, ch) for t in terms)


def solution(mesh):
    maps = P("dp", "lat", "lon", None)
    kernel = P(None, None, "dp", None)
    return jax.shard_map(
        body,
        mesh=mesh,
        in_specs=(maps, kernel, kernel, kernel, maps),
        out_specs=(maps, maps, kernel, kernel, kernel),
        check_vma=False,
    )
```
